512 devices in a mesh: rep: 4 (over y_hi, core), fsdp: 32 (over z, y_lo), tp: 4 (over x).
Axes of the slice: x: 4, y: 4 (y_hi: 2, y_lo: 2; y = y_hi * 2 + y_lo), z: 16, core: 2. Of those that a mesh axis runs over, the one named last changes fastest.
Arguments:
- master: float32 [128, 32, 14336], P(('rep', 'fsdp'), 'tp'), may hold values from -0.06 to 0.06
- moment_one: float32 [128, 32, 14336], P(('rep', 'fsdp'), 'tp'), may hold values from -2 to 2
- moment_two: float32 [128, 32, 14336], P(('rep', 'fsdp'), 'tp'), may hold values from 0.001 to 0.01
- grads: bfloat16 [4, 4, 32, 32, 14336], P('rep', None, 'fsdp', 'tp'), may hold values from -6 to 6
- inputs: bfloat16 [1024, 4096], P('fsdp'), may hold values from -6 to 6
- out_grad: bfloat16 [1024, 14336], P('fsdp', 'tp'), may hold values from -6 to 6
Outputs:
- new_master: float32 [128, 32, 14336], P(('rep', 'fsdp'), 'tp')
- new_one: float32 [128, 32, 14336], P(('rep', 'fsdp'), 'tp')
- new_two: float32 [128, 32, 14336], P(('rep', 'fsdp'), 'tp')
- forward_part: bfloat16 [4, 4, 1024, 14336], P('rep', 'tp', 'fsdp')
- backward_part: bfloat16 [4, 1024, 4096], P('tp', 'fsdp', 'rep')
The draws below stay inside these ranges and needn't reach their ends.
All inputs are finite; a program needn't handle non-finite values.
Results may differ from the reference program's by a relative error of at most 0.019.
Values may be sent and summed in bfloat16 or wider, within the bound.
A program may use at most 128 MiB of HBM per device.

```python
import math
import jax
import jax.numpy as jnp
from jax import lax

FF = 14336
ROWS_DEV = 8
BAND = 32
BANDS = 128
ROWS = 4096
TOKENS = 1024
N_REP = 4
N_FSDP = 32
N_TP = 4


def draw_master(key, part):
    key = jax.random.fold_in(key, 11)
    first, second, third = jax.random.split(key, 3)
    spread = math.sqrt(10.0)
    base = jnp.clip(jax.random.normal(first, (BANDS, BAND, FF), jnp.float32), -4.0, 4.0) * 0.0015
    row_scale = jnp.exp(jax.random.uniform(second, (BANDS, BAND, 1), jnp.float32) * math.log(spread))
    col_scale = jnp.exp(jax.random.uniform(third, (1, 1, FF), jnp.float32) * math.log(spread))
    return (base * row_scale * col_scale).astype(jnp.float32)


def block_scale(stream_key, dims, cuts, smallest, largest):
    loudness = 1.0
    for position, blocks in cuts:
        draws = jax.random.uniform(jax.random.fold_in(jax.random.fold_in(stream_key, 6), position), (blocks,), jnp.float32, smallest / len(cuts), largest / len(cuts))
        loudness = loudness * jnp.repeat(jnp.exp(draws), dims[position] // blocks).reshape((-1,) + (1,) * (len(dims) - 1 - position))
    return loudness


def centred(stream_key, extent, scale, limit, pieces=(), kind=jnp.bfloat16):
    loudness = block_scale(stream_key, extent, pieces, -0.22, 0.18) if pieces else 1.0
    drawn = jax.random.normal(stream_key, extent, jnp.float32) * scale * loudness
    return jnp.minimum(jnp.maximum(drawn, -limit), limit).astype(kind)


def setup_inputs(seed: int = 0) -> dict:
    streams_of = jax.random.split(jax.random.key(seed), 7)
    master = draw_master(jax.random.fold_in(streams_of[6], 71), 0)
    moment_one = centred(streams_of[1], (BANDS, BAND, FF), 0.3, 2.0, ((0, 128), (1, 4)), jnp.float32)
    moment_two = jnp.clip(jnp.exp(math.log(0.01) - 2.30258502 * jax.random.uniform(streams_of[2], (BANDS, BAND, FF), jnp.float32) ** block_scale(streams_of[2], (BANDS, BAND, FF), ((0, 128), (1, 4)), -0.2, 0.2)), 0.001, 0.01)
    grads = centred(streams_of[3], (N_REP, N_REP, N_FSDP, BAND, FF), 1.0, 6.0, ((0, 4), (2, 32), (3, 4)))
    inputs = centred(streams_of[4], (TOKENS, ROWS), 1.0, 6.0, ((0, 32),))
    out_grad = centred(streams_of[5], (TOKENS, FF), 1.0, 6.0, ((0, 32), (1, 4)))
    return dict(master=master, moment_one=moment_one, moment_two=moment_two, grads=grads, inputs=inputs, out_grad=out_grad)


beta_one = 0.9
beta_two = 0.95
learn_rate = 0.003
decay_rate = 0.1
block_width = 32

def reference(master, moment_one, moment_two, grads, inputs, out_grad):
    grad = lax.optimization_barrier(jnp.sum(grads.astype(jnp.float32), axis=0)).reshape(BANDS, BAND, FF) / N_REP
    new_one = beta_one * moment_one + (1.0 - beta_one) * grad
    new_two = beta_two * moment_two + (1.0 - beta_two) * grad * grad
    fix_one = 1.0 - beta_one ** 10
    fix_two = 1.0 - beta_two ** 10
    step_dir = new_one / fix_one / (jnp.sqrt(new_two / fix_two) + 1e-08)
    new_master = master - learn_rate * (step_dir + decay_rate * master)
    band_level = 2.5 * lax.optimization_barrier(jnp.mean(jnp.abs(new_master), axis=1, keepdims=True))
    band_copy = jnp.clip(new_master, -band_level, band_level).astype(jnp.bfloat16)
    blocks = new_master.reshape(BANDS, BAND, FF // block_width, block_width)
    unit_level = 2.5 * lax.optimization_barrier(jnp.mean(jnp.abs(blocks), axis=3, keepdims=True))
    unit_copy = jnp.clip(blocks, -unit_level, unit_level).reshape(BANDS, BAND, FF).astype(jnp.bfloat16)
    x_view = inputs.reshape(TOKENS, N_REP, N_FSDP, N_TP, ROWS_DEV)
    w_view = band_copy.reshape(N_REP, N_FSDP, N_TP, ROWS_DEV, FF)
    outer = []
    for group in range(N_REP):
        inner = []
        for tensor in range(N_TP):
            left = x_view[:, group, :, tensor, :].reshape(TOKENS, N_FSDP * ROWS_DEV)
            right = w_view[group, :, tensor].reshape(N_FSDP * ROWS_DEV, FF)
            inner.append(jnp.dot(left, right, preferred_element_type=jnp.float32).astype(jnp.bfloat16))
        outer.append(jnp.stack(inner))
    forward_part = jnp.stack(outer)
    unit_flat = unit_copy.reshape(ROWS, FF)
    quarter = FF // N_TP
    parts = []
    for tensor in range(N_TP):
        lhs = out_grad[:, tensor * quarter:(tensor + 1) * quarter]
        rhs = unit_flat[:, tensor * quarter:(tensor + 1) * quarter]
        parts.append(jnp.dot(lhs, rhs.T, preferred_element_type=jnp.float32).astype(jnp.bfloat16))
    backward_part = jnp.stack(parts)
    return (new_master, new_one, new_two, forward_part, backward_part)
```

```python
import functools

import jax
import jax.numpy as jnp
from jax import lax
from jax.experimental import pallas as pl
from jax.experimental.pallas import tpu as pltpu
from jax.sharding import PartitionSpec as P

beta_one = 0.9
beta_two = 0.95
learn_rate = 0.003
decay_rate = 0.1
block_width = 32

MESH = pl.DeviceIdType.MESH
F32 = jnp.float32
BF16 = jnp.bfloat16

UNIT = 1024
MSG = UNIT + 128
LEAD = 3


def kernel(
    nz, nu,
    master, mone, mtwo, grads, inputs, ograd,
    o_master, o_one, o_two, o_fwd, o_bwd,
    m0, m1, m2, gr, xa, xs, ogb, sel, ones,
    sa, ra, keep, sb, rb, ys, yr, ps, pr, g, fo, acc, bs, br, bo,
    ld, sa_s, sa_r, sb_s, sb_r, ys_s, ys_r, ps_s, ps_r, ring_s, ring_r,
    og_s, og_r, sh_s, sh_r, xs_s, xs_r, fo_s, fo_r, fo_l, bw_s, bw_r, out_s,
):
    half = nu * UNIT
    rep = lax.axis_index("rep")
    fs = lax.axis_index("fsdp")
    t = lax.axis_index("tp")
    nf = 2 * nz
    yh = lax.div(rep, 2)
    k = lax.rem(rep, 2)
    z = lax.div(fs, 2)
    y = lax.rem(fs, 2)
    first_core = k == 0
    first_y = y == 0

    sibling = {"rep": rep + 1 - 2 * k}
    opposite = {"rep": lax.rem(rep + 2, 4)}
    up = {"fsdp": lax.rem(fs + 2, nf)}
    down = {"fsdp": lax.rem(fs + nf - 2, nf)}
    mate = {"fsdp": fs + 1 - 2 * y}
    plane = [(dx, dy) for dx in range(4) for dy in range(2) if (dx, dy) != (0, 0)]

    def at(dx, dy):
        where_to = {}
        if dx:
            where_to["tp"] = lax.rem(t + dx, 4)
        if dy:
            where_to["fsdp"] = fs + 1 - 2 * y
        return where_to

    def remote(src, dst, send, recv, who):
        return pltpu.make_async_remote_copy(
            src_ref=src, dst_ref=dst, send_sem=send, recv_sem=recv, device_id=who, device_id_type=MESH
        )

    def aligned(value, step):
        return pl.multiple_of(value, step)

    loads = [
        pltpu.make_async_copy(grads, gr, ld.at[0]),
        pltpu.make_async_copy(master, m0, ld.at[1]),
        pltpu.make_async_copy(mone, m1, ld.at[2]),
        pltpu.make_async_copy(mtwo, m2, ld.at[3]),
        pltpu.make_async_copy(inputs.at[:, pl.ds(aligned(rep * 1024, 1024), 1024)], xa, ld.at[4]),
    ]
    for load in loads:
        load.start()
    barrier = pltpu.get_barrier_semaphore()
    partners = [sibling, opposite, up, down] + [at(dx, dy) for dx, dy in plane]
    for who in partners:
        pl.semaphore_signal(barrier, inc=1, device_id=who, device_id_type=MESH)
    row_of = lax.broadcasted_iota(jnp.int32, (256, 256), 0)
    col_of = lax.broadcasted_iota(jnp.int32, (256, 256), 1)
    ones[...] = jnp.where(lax.div(row_of, block_width) == lax.div(col_of, block_width), 1.0, 0.0).astype(BF16)
    for q in range(4):
        target = lax.div(row_of, 8) * 32 + t * 8 + lax.rem(row_of, 8)
        sel[:, q * 256:(q + 1) * 256] = jnp.where(target == col_of + q * 256, 1.0, 0.0).astype(BF16)
    acc[...] = jnp.zeros_like(acc)
    loads[0].wait()
    pl.semaphore_wait(barrier, len(partners))

    def copy_a(u):
        return remote(sa.at[u], ra.at[u], sa_s.at[u], sa_r.at[u], sibling)

    def two_groups(hi, cols):
        pair = gr[pl.ds(aligned(hi * 16, 16), 16), cols].astype(F32)
        return pair[0:8], pair[8:16]

    def stage_a(u, carry):
        for h in range(2):
            cols = pl.ds(aligned(h * half + u * UNIT, UNIT), UNIT)
            a0, a1 = two_groups(yh, cols)
            b0, b1 = two_groups(1 - yh, cols)
            kept = jnp.where(first_core, a1, a0)
            sent = jnp.where(first_core, b1, b0)
            sa[u, :, h * UNIT:(h + 1) * UNIT] = jnp.concatenate([kept, sent], axis=0).astype(BF16)
        copy_a(u).start()
        return carry

    lax.fori_loop(0, nu, stage_a, 0)

    loads[4].wait()
    mine = lax.dot_general(xa[...], sel[...], (((1,), (1,)), ((), ())), preferred_element_type=F32).astype(BF16)
    my_rows = pl.ds(aligned(y * 32, 32), 32)
    xs[my_rows, :] = mine
    copy_x = remote(xs.at[my_rows, :], xs.at[my_rows, :], xs_s, xs_r, mate)
    copy_x.start()
    for load in loads[1:4]:
        load.wait()

    def copy_b(u):
        return remote(sb.at[u], rb.at[u], sb_s.at[u], sb_r.at[u], opposite)

    def stage_b(u):
        copy_a(u).wait_recv()
        sends = []
        for h in range(2):
            cols = pl.ds(aligned(h * half + u * UNIT, UNIT), UNIT)
            a0, a1 = two_groups(yh, cols)
            b0, b1 = two_groups(1 - yh, cols)
            got = ra[u, :, h * UNIT:(h + 1) * UNIT].astype(F32)
            keep[u, :, h * UNIT:(h + 1) * UNIT] = jnp.where(first_core, a0, a1) + got[0:8]
            sends.append(jnp.where(first_core, b0, b1) + got[8:16])
        sb[u] = jnp.concatenate(sends, axis=0).astype(BF16)
        copy_b(u).start()

    def copy_y(u):
        return remote(ys.at[u], yr.at[u], ys_s.at[u], ys_r.at[u], mate)

    def copy_p(u, dx, dy):
        mine = t * 2 + y
        choice = y if dy == 0 else 1 - y
        return remote(ps.at[u, choice], pr.at[u, mine], ps_s.at[u, dx * 2 + dy], ps_r.at[u, mine], at(dx, dy))

    def wait_p(u, dx, dy):
        slot = lax.rem(t + dx, 4) * 2 + (y if dy == 0 else 1 - y)
        remote(ps.at[u, 0], pr.at[u, slot], ps_s.at[u, dx * 2 + dy], ps_r.at[u, slot], at(dx, dy)).wait_recv()

    fix_one = 1.0 - beta_one**10
    fix_two = 1.0 - beta_two**10
    sub = lax.broadcasted_iota(jnp.int32, (8, 128), 0)

    def stage_c(u):
        copy_b(u).wait_recv()
        got = rb[u].astype(F32)
        for h in range(2):
            cols = pl.ds(aligned(h * half + u * UNIT, UNIT), UNIT)
            grad = (keep[u, :, h * UNIT:(h + 1) * UNIT] + got[h * 8:(h + 1) * 8]) * 0.25
            new_one = beta_one * m1[:, cols] + (1.0 - beta_one) * grad
            new_two = beta_two * m2[:, cols] + (1.0 - beta_two) * grad * grad
            step_dir = new_one / fix_one / (jnp.sqrt(new_two / fix_two) + 1e-08)
            old = m0[:, cols]
            new = old - learn_rate * (step_dir + decay_rate * old)
            m0[:, cols] = new
            m1[:, cols] = new_one
            m2[:, cols] = new_two
            total = jnp.sum(jnp.abs(new), axis=0, keepdims=True)
            packed = jnp.zeros((8, 128), F32)
            for r in range(8):
                packed = jnp.where(sub == r, total[:, r * 128:(r + 1) * 128], packed)
            ps[u, h] = packed
        pr[u, t * 2 + y] = ps[u, y]
        for dx, dy in plane:
            copy_p(u, dx, dy).start()
        other = m0[:, pl.ds(aligned((1 - y) * half + u * UNIT, UNIT), UNIT)]
        ys[u] = jnp.concatenate([other[:, :UNIT // 2], other[:, UNIT // 2:]], axis=0).astype(BF16)
        copy_y(u).start()

    def stage_d(u):
        for dx, dy in plane:
            wait_p(u, dx, dy)
        levels = []
        for e in range(2):
            total = pr[u, e] + pr[u, 2 + e] + pr[u, 4 + e] + pr[u, 6 + e]
            levels.append(total * (2.5 / 32.0))
        g[z, :, pl.ds(aligned(u * MSG + UNIT, 128), 128)] = jnp.concatenate(levels, axis=0).astype(BF16)
        copy_y(u).wait_recv()
        got = yr[u].astype(F32)
        theirs = jnp.concatenate([got[0:8], got[8:16]], axis=1)
        own = m0[:, pl.ds(aligned(y * half + u * UNIT, UNIT), UNIT)]
        even = jnp.where(first_y, own, theirs)
        odd = jnp.where(first_y, theirs, own)
        g[z, :, pl.ds(aligned(u * MSG, 128), UNIT)] = jnp.concatenate([even, odd], axis=0).astype(BF16)

    def place(c, src):
        return g.at[src, :, pl.ds(aligned(c * MSG, 128), MSG)]

    def ring(c, s, src, way, who):
        return remote(place(c, src), place(c, src), ring_s.at[way, c, s], ring_r.at[c, src], who)

    def arrived(c, src):
        ring(c, 0, src, 0, up).wait_recv()

    def ring_step(c, s):
        below = lax.rem(z + nz - s, nz)
        above = lax.rem(z + s, nz)
        last = nz // 2 - 1
        if s > 0:
            arrived(c, below)
            if s < last:
                ring(c, s, below, 0, up).start()
            arrived(c, above)
        else:
            ring(c, s, below, 0, up).start()
        if s < last:
            ring(c, s, above, 1, down).start()
        else:
            even = lax.rem(c, 2) == 0
            src = jnp.where(even, below, above)
            to = jnp.where(even, lax.rem(fs + 2, nf), lax.rem(fs + nf - 2, nf))
            ring(c, s, src, 0, {"fsdp": to}).start()

    def og_slot(xsrc, ysrc, core):
        return ogb.at[lax.rem(xsrc, 2), pl.ds(aligned(ysrc * 32 + core * 16, 16), 16), :]

    og_from = ograd.at[pl.ds(aligned(k * 16, 16), 16), :]
    og_row = lax.div(t, 2)
    og_number = lax.rem(t, 2) * 2 + y

    def og_send():
        for dx in range(4):
            to = {"tp": lax.rem(t + dx, 4), "fsdp": fs - y + og_row}
            dst = og_slot(t, y, k)
            if dx == 0:
                @pl.when(og_row == y)
                def _():
                    pltpu.make_async_copy(og_from, dst, og_r.at[og_number]).start()

                @pl.when(og_row != y)
                def _():
                    remote(og_from, dst, og_s.at[dx], og_r.at[og_number], to).start()
            else:
                remote(og_from, dst, og_s.at[dx], og_r.at[og_number], to).start()

    def og_share(i):
        slot = og_slot(2 * y + i // 2, i % 2, k)
        return remote(slot, slot, sh_s.at[i], sh_r.at[i], sibling)

    def og_pass():
        for i in range(4):
            slot = og_slot(2 * y + i // 2, i % 2, k)
            local = jnp.logical_and(t == 2 * y + i // 2, y == i % 2)

            @pl.when(local)
            def _():
                pltpu.make_async_copy(og_from, slot, og_r.at[i]).wait()

            @pl.when(jnp.logical_not(local))
            def _():
                remote(og_from, slot, og_s.at[0], og_r.at[i], mate).wait_recv()

            og_share(i).start()

    def og_finish():
        for i in range(4):
            slot = og_slot(2 * y + i // 2, i % 2, 1 - k)
            remote(slot, slot, sh_s.at[i], sh_r.at[i], sibling).wait_recv()
        other_rows = pl.ds(aligned((1 - y) * 32, 32), 32)
        remote(xs.at[other_rows, :], xs.at[other_rows, :], xs_s, xs_r, mate).wait_recv()

    def fo_cols(u, side):
        return pl.ds(aligned(side * half + u * UNIT, UNIT), UNIT)

    def fo_local(u):
        return pltpu.make_async_copy(fo.at[u, my_rows, :], o_fwd.at[:, fo_cols(u, y)], fo_l.at[u])

    def fo_remote(u, side):
        rows = pl.ds(aligned((1 - y) * 32, 32), 32)
        return remote(fo.at[u, rows, :], o_fwd.at[:, fo_cols(u, side)], fo_s.at[u], fo_r.at[u], mate)

    def products(u, low, high):
        levels = g[:, :, pl.ds(aligned(u * MSG + UNIT, 128), 128)].astype(F32).reshape(2 * nz, 8, 128)
        for i in range(low, high):
            b = 4 * u + i
            whole = g[:, :, pl.ds(aligned(u * MSG + i * 256, 128), 256)].reshape(16 * nz, 256)
            wide = whole.astype(F32)
            spread = [
                jnp.broadcast_to(levels[:, r:r + 1, :], (2 * nz, 8, 128)).reshape(16 * nz, 128)
                for r in (2 * i, 2 * i + 1)
            ]
            level = jnp.concatenate(spread, axis=1)
            band = jnp.maximum(jnp.minimum(wide, level), -level).astype(BF16)
            fwd = jnp.dot(xs[...], band, preferred_element_type=F32)
            fo[u, :, i * 256:(i + 1) * 256] = fwd.astype(BF16)
            sums = jnp.dot(jnp.abs(whole), ones[...], preferred_element_type=F32)
            level = sums * (2.5 / 32.0)
            unit = jnp.maximum(jnp.minimum(wide, level), -level).astype(BF16)
            hg = lax.div(b, 2 * nu)
            og = ogb[hg, :, pl.ds(aligned((b - hg * 2 * nu) * 256, 256), 256)]
            acc[hg] += lax.dot_general(og, unit, (((1,), (1,)), ((), ())), preferred_element_type=F32)

    def results(u):
        fo_local(u).start()
        fo_remote(u, y).start()

    outs = [
        pltpu.make_async_copy(m0, o_master, out_s.at[0]),
        pltpu.make_async_copy(m1, o_one, out_s.at[1]),
        pltpu.make_async_copy(m2, o_two, out_s.at[2]),
    ]
    steps = nz // 2
    rounds = (steps + LEAD - 1) // LEAD

    ahead = 3

    def one_round(q, carry):
        def guarded(back, body):
            @pl.when(jnp.logical_and(q >= ahead + back, q < ahead + back + nu))
            def _():
                body(lax.rem(q + 4 * nu - ahead - back, nu))

        def once(number, body):
            pl.when(q == ahead + number)(body)

        def first_products(c):
            arrived(c, lax.rem(z + nz // 2, nz))
            products(c, 0, 2)

        def last_products(c):
            products(c, 2, 4)
            results(c)

        def write_out():
            for out in outs:
                out.start()

        for j in range(LEAD):
            if j == 0:
                guarded(0, stage_d)
            for i in reversed(range(rounds)):
                s = i * LEAD + j
                if s < steps:
                    guarded(i, functools.partial(ring_step, s=s))
            if j == LEAD - 1:
                once(0, og_send)
                once(1, og_pass)
                once(2, og_finish)
                guarded(rounds - 1, first_products)
            if j == 0:
                guarded(rounds, last_products)
            if j == 1:
                guarded(-3, stage_b)
            if j == 2:
                guarded(-2, stage_c)
                once(nu - 3, write_out)
        return carry

    lax.fori_loop(0, ahead + nu + rounds - 1, one_round, 0)
    products(nu - 1, 2, 4)
    results(nu - 1)

    for hg in range(2):
        rows = acc[hg].astype(BF16)
        bs[hg] = jnp.dot(rows, sel[...], preferred_element_type=F32).astype(BF16)

    def bw_send(hg, yy):
        return remote(
            bs.at[hg, pl.ds(yy * 32, 32), :], br.at[t], bw_s.at[hg * 2 + yy], bw_r.at[t],
            {"tp": 2 * y + hg, "fsdp": fs - y + yy},
        )

    def is_self(hg, yy):
        return jnp.logical_and(t == 2 * y + hg, y == yy)

    for hg in range(2):
        for yy in range(2):
            @pl.when(is_self(hg, yy))
            def _():
                br[t] = bs[hg, yy * 32:(yy + 1) * 32, :]

            @pl.when(jnp.logical_not(is_self(hg, yy)))
            def _():
                bw_send(hg, yy).start()

    at_home = lax.div(t, 2) == y
    for x in range(4):
        @pl.when(jnp.logical_not(jnp.logical_and(at_home, t == x)))
        def _():
            remote(
                bs.at[0, pl.ds(0, 32), :], br.at[x], bw_s.at[0], bw_r.at[x], mate
            ).wait_recv()
    total = br[0].astype(F32) + br[1].astype(F32) + br[2].astype(F32) + br[3].astype(F32)
    bo[...] = total.astype(BF16)
    out_b = pltpu.make_async_copy(bo, o_bwd, out_s.at[3])
    out_b.start()

    for hg in range(2):
        for yy in range(2):
            @pl.when(jnp.logical_not(is_self(hg, yy)))
            def _():
                bw_send(hg, yy).wait_send()
    for dx in range(4):
        def og_done():
            remote(og_from, og_slot(t, y, k), og_s.at[dx], og_r.at[og_number], mate).wait_send()
        if dx == 0:
            pl.when(og_row != y)(og_done)
        else:
            og_done()
    for i in range(4):
        og_share(i).wait_send()
    copy_x.wait_send()

    def finish(u, carry):
        copy_a(u).wait_send()
        copy_b(u).wait_send()
        copy_y(u).wait_send()
        for dx, dy in plane:
            copy_p(u, dx, dy).wait_send()
        for s in range(steps):
            ring(u, s, z, 0, up).wait_send()
            if s < steps - 1:
                ring(u, s, z, 1, down).wait_send()
        fo_local(u).wait()
        fo_remote(u, y).wait_send()
        fo_remote(u, 1 - y).wait_recv()
        return carry

    lax.fori_loop(0, nu, finish, 0)
    for out in outs:
        out.wait()
    out_b.wait()


def local(master, moment_one, moment_two, grads, inputs, out_grad):
    nz = lax.axis_size("fsdp") // 2
    rows, hidden = master.shape[1:]
    tokens = inputs.shape[0]
    nu = hidden // 2 // UNIT
    steps = nz // 2
    any_spec = pl.BlockSpec(memory_space=pl.ANY)
    vm = pltpu.VMEM
    dma = pltpu.SemaphoreType.DMA
    new_master, new_one, new_two, fwd, bwd = pl.pallas_call(
        functools.partial(kernel, nz, nu),
        out_shape=(
            jax.ShapeDtypeStruct((rows, hidden), F32),
            jax.ShapeDtypeStruct((rows, hidden), F32),
            jax.ShapeDtypeStruct((rows, hidden), F32),
            jax.ShapeDtypeStruct((tokens, hidden), BF16),
            jax.ShapeDtypeStruct((tokens, 64 * nz), BF16),
        ),
        in_specs=[any_spec] * 6,
        out_specs=[any_spec] * 5,
        scratch_shapes=[
            vm((rows, hidden), F32),
            vm((rows, hidden), F32),
            vm((rows, hidden), F32),
            vm((32, hidden), BF16),
            vm((tokens, 64 * nz), BF16),
            vm((2 * tokens, 16 * nz), BF16),
            vm((2, 2 * tokens, hidden // 4), BF16),
            vm((16 * nz, 64 * nz), BF16),
            vm((256, 256), BF16),
            vm((nu, 16, 2 * UNIT), BF16),
            vm((nu, 16, 2 * UNIT), BF16),
            vm((nu, 8, 2 * UNIT), F32),
            vm((nu, 16, UNIT), BF16),
            vm((nu, 16, UNIT), BF16),
            vm((nu, 16, UNIT // 2), BF16),
            vm((nu, 16, UNIT // 2), BF16),
            vm((nu, 2, 8, 128), F32),
            vm((nu, 8, 8, 128), F32),
            vm((nz, 16, nu * MSG), BF16),
            vm((nu, 2 * tokens, UNIT), BF16),
            vm((2, 2 * tokens, 16 * nz), F32),
            vm((2, 2 * tokens, 64 * nz), BF16),
            vm((4, tokens, 64 * nz), BF16),
            vm((tokens, 64 * nz), BF16),
            dma((5,)),
            dma((nu,)), dma((nu,)), dma((nu,)), dma((nu,)), dma((nu,)), dma((nu,)),
            dma((nu, 8)), dma((nu, 8)),
            dma((2, nu, steps)), dma((nu, nz)),
            dma((4,)), dma((4,)), dma((4,)), dma((4,)),
            dma, dma,
            dma((nu,)), dma((nu,)), dma((nu,)),
            dma((4,)), dma((4,)),
            dma((4,)),
        ],
        compiler_params=pltpu.CompilerParams(
            collective_id=0, has_side_effects=True, vmem_limit_bytes=48 * 1024 * 1024
        ),
    )(
        master.reshape(rows, hidden),
        moment_one.reshape(rows, hidden),
        moment_two.reshape(rows, hidden),
        grads.reshape(32, hidden),
        inputs,
        out_grad,
    )
    return (
        new_master.reshape(master.shape),
        new_one.reshape(master.shape),
        new_two.reshape(master.shape),
        fwd.reshape(1, 1, tokens, hidden),
        bwd.reshape(1, tokens, 64 * nz),
    )


def solution(mesh):
    placed = (
        P(("rep", "fsdp"), "tp", None),
        P(("rep", "fsdp"), "tp", None),
        P(("rep", "fsdp"), "tp", None),
        P("rep", None, "fsdp", "tp", None),
        P("fsdp", None),
        P("fsdp", "tp"),
    )
    return jax.shard_map(
        local,
        mesh=mesh,
        in_specs=placed,
        out_specs=(
            P(("rep", "fsdp"), "tp", None),
            P(("rep", "fsdp"), "tp", None),
            P(("rep", "fsdp"), "tp", None),
            P("rep", "tp", "fsdp", None),
            P("tp", "fsdp", "rep"),
        ),
        check_vma=False,
    )
```

```python
import functools

import jax
import jax.numpy as jnp
from jax import lax
from jax.experimental import pallas as pl
from jax.experimental.pallas import tpu as pltpu
from jax.sharding import PartitionSpec as P

beta_one = 0.9
beta_two = 0.95
learn_rate = 0.003
decay_rate = 0.1
block_width = 32

MESH = pl.DeviceIdType.MESH
F32 = jnp.float32
BF16 = jnp.bfloat16

VMEM_BYTES = 63 * 1024 * 1024
UNIT = 1792
BLOCKS = UNIT // 256
MSG = UNIT + 256


def kernel(
    nz, nu,
    master, mone, mtwo, grads, inputs, ograd,
    o_master, o_one, o_two, o_fwd, o_bwd,
    m0, m1, m2, gr, xa, xs, xk, ogb, sel, ones,
    sa, ra, keep, sb, rb, ys, yr, ps, pr, g, facc, fo, acc, bs, br, bo,
    ld, sa_s, sa_r, sb_s, sb_r, ys_s, ys_r, ps_s, ps_r, ring_s, ring_r,
    og_s, og_r, sh_s, sh_r, xs_s, xs_r, fo_s, fo_r, fo_l, bw_s, bw_r, out_s,
):
    half = nu * UNIT
    rep = lax.axis_index("rep")
    fs = lax.axis_index("fsdp")
    t = lax.axis_index("tp")
    nf = 2 * nz
    yh = lax.div(rep, 2)
    k = lax.rem(rep, 2)
    z = lax.div(fs, 2)
    y = lax.rem(fs, 2)
    first_core = k == 0
    first_y = y == 0

    sibling = {"rep": rep + 1 - 2 * k}
    opposite = {"rep": lax.rem(rep + 2, 4)}
    up = {"fsdp": lax.rem(fs + 2, nf)}
    down = {"fsdp": lax.rem(fs + nf - 2, nf)}
    mate = {"fsdp": fs + 1 - 2 * y}
    plane = [(dx, dy) for dx in range(4) for dy in range(2) if (dx, dy) != (0, 0)]

    def at(dx, dy):
        where_to = {}
        if dx:
            where_to["tp"] = lax.rem(t + dx, 4)
        if dy:
            where_to["fsdp"] = fs + 1 - 2 * y
        return where_to

    def remote(src, dst, send, recv, who):
        return pltpu.make_async_remote_copy(
            src_ref=src, dst_ref=dst, send_sem=send, recv_sem=recv, device_id=who, device_id_type=MESH
        )

    def aligned(value, step):
        return pl.multiple_of(value, step)

    loads = [
        pltpu.make_async_copy(grads, gr, ld.at[0]),
        pltpu.make_async_copy(master, m0, ld.at[1]),
        pltpu.make_async_copy(mone, m1, ld.at[2]),
        pltpu.make_async_copy(mtwo, m2, ld.at[3]),
        pltpu.make_async_copy(inputs.at[:, pl.ds(aligned(rep * 1024, 1024), 1024)], xa, ld.at[4]),
    ]
    barrier = pltpu.get_barrier_semaphore()
    partners = [sibling, opposite, up, down] + [at(dx, dy) for dx, dy in plane]
    for who in partners:
        pl.semaphore_signal(barrier, inc=1, device_id=who, device_id_type=MESH)
    for load in loads:
        load.start()
    loads[0].wait()
    pl.semaphore_wait(barrier, len(partners))

    def copy_a(u):
        return remote(sa.at[u], ra.at[u], sa_s.at[u], sa_r.at[u], sibling)

    def two_groups(hi, cols):
        pair = gr[pl.ds(aligned(hi * 16, 16), 16), cols].astype(F32)
        return pair[0:8], pair[8:16]

    def stage_a(u, carry):
        for h in range(2):
            cols = pl.ds(aligned(h * half + u * UNIT, 256), UNIT)
            a0, a1 = two_groups(yh, cols)
            b0, b1 = two_groups(1 - yh, cols)
            kept = jnp.where(first_core, a1, a0)
            sent = jnp.where(first_core, b1, b0)
            sa[u, :, h * UNIT:(h + 1) * UNIT] = jnp.concatenate([kept, sent], axis=0).astype(BF16)
        copy_a(u).start()
        return carry

    lax.fori_loop(0, nu, stage_a, 0)

    my_rows = pl.ds(aligned(y * 32, 32), 32)
    copy_x = remote(xs.at[my_rows, :], xs.at[my_rows, :], xs_s, xs_r, mate)

    def choose():
        row_of = lax.broadcasted_iota(jnp.int32, (256, 256), 0)
        col_of = lax.broadcasted_iota(jnp.int32, (256, 256), 1)
        ones[...] = jnp.where((row_of >> 5) == (col_of >> 5), 1.0, 0.0).astype(BF16)
        slot = row_of >> 4
        away = (slot + 1) >> 1
        band = 2 * (jnp.where((slot & 1) == 1, z + nz - away, z + away) & (nz - 1)) + ((row_of >> 3) & 1)
        target = band * 32 + t * 8 + (row_of & 7)
        for q in range(4):
            sel[:, q * 256:(q + 1) * 256] = jnp.where(target == col_of + q * 256, 1.0, 0.0).astype(BF16)
        acc[...] = jnp.zeros_like(acc)
        loads[4].wait()
        mine = lax.dot_general(xa[...], sel[...], (((1,), (1,)), ((), ())), preferred_element_type=F32)
        xs[my_rows, :] = mine.astype(BF16)
        copy_x.start()

    def copy_b(u):
        return remote(sb.at[u], rb.at[u], sb_s.at[u], sb_r.at[u], opposite)

    def stage_b(u):
        copy_a(u).wait_recv()
        sends = []
        for h in range(2):
            cols = pl.ds(aligned(h * half + u * UNIT, 256), UNIT)
            a0, a1 = two_groups(yh, cols)
            b0, b1 = two_groups(1 - yh, cols)
            got = ra[u, :, h * UNIT:(h + 1) * UNIT].astype(F32)
            keep[u, :, h * UNIT:(h + 1) * UNIT] = jnp.where(first_core, a0, a1) + got[0:8]
            sends.append(jnp.where(first_core, b0, b1) + got[8:16])
        sb[u] = jnp.concatenate(sends, axis=0).astype(BF16)
        copy_b(u).start()

    def copy_y(u):
        return remote(ys.at[u], yr.at[u], ys_s.at[u], ys_r.at[u], mate)

    def copy_p(u, dx, dy):
        mine = t * 2 + y
        choice = y if dy == 0 else 1 - y
        return remote(ps.at[u, choice], pr.at[u, mine], ps_s.at[u, dx * 2 + dy], ps_r.at[u, mine], at(dx, dy))

    def wait_p(u, dx, dy):
        slot = lax.rem(t + dx, 4) * 2 + (y if dy == 0 else 1 - y)
        remote(ps.at[u, 0], pr.at[u, slot], ps_s.at[u, dx * 2 + dy], ps_r.at[u, slot], at(dx, dy)).wait_recv()

    scale_one = 1.0 / (1.0 - beta_one**10)
    scale_two = 1.0 / (1.0 - beta_two**10)
    sub = lax.broadcasted_iota(jnp.int32, (8, 256), 0)

    def stage_c(u):
        copy_b(u).wait_recv()
        got = rb[u].astype(F32)
        for h in range(2):
            cols = pl.ds(aligned(h * half + u * UNIT, 256), UNIT)
            grad = (keep[u, :, h * UNIT:(h + 1) * UNIT] + got[h * 8:(h + 1) * 8]) * 0.25
            new_one = beta_one * m1[:, cols] + (1.0 - beta_one) * grad
            new_two = beta_two * m2[:, cols] + (1.0 - beta_two) * grad * grad
            step_dir = new_one * scale_one / (jnp.sqrt(new_two * scale_two) + 1e-08)
            old = m0[:, cols]
            new = old - learn_rate * (step_dir + decay_rate * old)
            m0[:, cols] = new
            m1[:, cols] = new_one
            m2[:, cols] = new_two
            total = jnp.sum(jnp.abs(new), axis=0, keepdims=True)
            packed = jnp.zeros((8, 256), F32)
            for r in range(BLOCKS):
                packed = jnp.where(sub == r, total[:, r * 256:(r + 1) * 256], packed)
            ps[u, h] = packed
        pr[u, t * 2 + y] = ps[u, y]
        for dx, dy in plane:
            copy_p(u, dx, dy).start()
        other = m0[:, pl.ds(aligned((1 - y) * half + u * UNIT, 256), UNIT)]
        ys[u] = jnp.concatenate([other[:, :UNIT // 2], other[:, UNIT // 2:]], axis=0).astype(BF16)
        copy_y(u).start()

    def stage_d(u):
        for dx, dy in plane:
            wait_p(u, dx, dy)
        levels = []
        for e in range(2):
            total = pr[u, e] + pr[u, 2 + e] + pr[u, 4 + e] + pr[u, 6 + e]
            levels.append(total * (2.5 / 32.0))
        g[0, :, pl.ds(aligned(u * MSG + UNIT, 256), 256)] = jnp.concatenate(levels, axis=0).astype(BF16)
        copy_y(u).wait_recv()
        got = yr[u].astype(F32)
        theirs = jnp.concatenate([got[0:8], got[8:16]], axis=1)
        own = m0[:, pl.ds(aligned(y * half + u * UNIT, 256), UNIT)]
        even = jnp.where(first_y, own, theirs)
        odd = jnp.where(first_y, theirs, own)
        g[0, :, pl.ds(aligned(u * MSG, 128), UNIT)] = jnp.concatenate([even, odd], axis=0).astype(BF16)

    def place(c, slot):
        return g.at[slot, :, pl.ds(aligned(c * MSG, 128), MSG)]

    def ring(c, s, way, who):
        src = max(2 * s - 1, 0) if way == 0 else 2 * s
        dst = min(2 * s + 1 + way, nz - 1)
        return remote(place(c, src), place(c, dst), ring_s.at[way, c, s], ring_r.at[c, dst], who)

    def arrived(c, slot):
        remote(place(c, slot), place(c, slot), ring_s.at[0, c, 0], ring_r.at[c, slot], up).wait_recv()

    def ring_step(c, s):
        if s > 0:
            arrived(c, 2 * s - 1)
        if s < steps - 1:
            ring(c, s, 0, up).start()
            if s > 0:
                arrived(c, 2 * s)
            ring(c, s, 1, down).start()
        else:
            arrived(c, 2 * s)

            @pl.when(lax.rem(c, 2) == 0)
            def _():
                ring(c, s, 0, up).start()

            @pl.when(lax.rem(c, 2) == 1)
            def _():
                ring(c, s, 1, down).start()

    def og_slot(xsrc, ysrc, core):
        return ogb.at[lax.rem(xsrc, 2), pl.ds(aligned(ysrc * 32 + core * 16, 16), 16), :]

    og_from = ograd.at[pl.ds(aligned(k * 16, 16), 16), :]
    og_row = lax.div(t, 2)
    og_number = lax.rem(t, 2) * 2 + y

    def og_send():
        for dx in range(4):
            to = {"tp": lax.rem(t + dx, 4), "fsdp": fs - y + og_row}
            dst = og_slot(t, y, k)
            if dx == 0:
                @pl.when(og_row == y)
                def _():
                    pltpu.make_async_copy(og_from, dst, og_r.at[og_number]).start()

                @pl.when(og_row != y)
                def _():
                    remote(og_from, dst, og_s.at[dx], og_r.at[og_number], to).start()
            else:
                remote(og_from, dst, og_s.at[dx], og_r.at[og_number], to).start()

    def og_share(i):
        slot = og_slot(2 * y + i // 2, i % 2, k)
        return remote(slot, slot, sh_s.at[i], sh_r.at[i], sibling)

    def og_pass():
        for i in range(4):
            slot = og_slot(2 * y + i // 2, i % 2, k)
            local = jnp.logical_and(t == 2 * y + i // 2, y == i % 2)

            @pl.when(local)
            def _():
                pltpu.make_async_copy(og_from, slot, og_r.at[i]).wait()

            @pl.when(jnp.logical_not(local))
            def _():
                remote(og_from, slot, og_s.at[0], og_r.at[i], mate).wait_recv()

            og_share(i).start()

    def og_finish():
        for i in range(4):
            slot = og_slot(2 * y + i // 2, i % 2, 1 - k)
            remote(slot, slot, sh_s.at[i], sh_r.at[i], sibling).wait_recv()
        other_rows = pl.ds(aligned((1 - y) * 32, 32), 32)
        remote(xs.at[other_rows, :], xs.at[other_rows, :], xs_s, xs_r, mate).wait_recv()
        for kk in range(4):
            xk[kk] = xs[:, kk * 64:(kk + 1) * 64]

    def fo_cols(u, side):
        return pl.ds(aligned(side * half + u * UNIT, 256), UNIT)

    def fo_local(u):
        return pltpu.make_async_copy(fo.at[u, my_rows, :], o_fwd.at[:, fo_cols(u, y)], fo_l.at[u])

    def fo_remote(u, side):
        rows = pl.ds(aligned((1 - y) * 32, 32), 32)
        return remote(fo.at[u, rows, :], o_fwd.at[:, fo_cols(u, side)], fo_s.at[u], fo_r.at[u], mate)

    def products(u, kk):
        slots = slice(4 * kk, 4 * kk + 4)
        levels = g[slots, :, pl.ds(aligned(u * MSG + UNIT, 256), 256)].astype(F32).reshape(8, 8, 256)
        wholes = [g[slots, :, pl.ds(aligned(u * MSG + i * 256, 256), 256)].reshape(64, 256) for i in range(BLOCKS)]
        sums = jnp.dot(jnp.abs(jnp.concatenate(wholes, axis=0)), ones[...], preferred_element_type=F32)
        hg = lax.div(u, 2)
        for i in range(BLOCKS):
            wide = wholes[i].astype(F32)
            level = jnp.broadcast_to(levels[:, i:i + 1, :], (8, 8, 256)).reshape(64, 256)
            band = jnp.maximum(jnp.minimum(wide, level), -level).astype(BF16)
            fwd = jnp.dot(xk[kk], band, preferred_element_type=F32)
            cols = slice(i * 256, (i + 1) * 256)
            if kk == 0:
                facc[u, :, cols] = fwd
            elif kk < 3:
                facc[u, :, cols] += fwd
            else:
                fo[u, :, cols] = (facc[u, :, cols] + fwd).astype(BF16)
            level = sums[i * 64:(i + 1) * 64] * (2.5 / 32.0)
            unit = jnp.maximum(jnp.minimum(wide, level), -level).astype(BF16)
            og = ogb[hg, :, pl.ds(aligned(lax.rem(u, 2) * UNIT + i * 256, 256), 256)]
            acc[hg, kk * 64:(kk + 1) * 64, :] += lax.dot_general(
                unit, og, (((1,), (1,)), ((), ())), preferred_element_type=F32
            )

    def results(u):
        fo_local(u).start()
        fo_remote(u, y).start()

    outs = [
        pltpu.make_async_copy(m0, o_master, out_s.at[0]),
        pltpu.make_async_copy(m1, o_one, out_s.at[1]),
        pltpu.make_async_copy(m2, o_two, out_s.at[2]),
    ]
    steps = nz // 2

    def bw_send(hg, yy):
        return remote(
            bs.at[hg, pl.ds(yy * 32, 32), :], br.at[t], bw_s.at[hg * 2 + yy], bw_r.at[t],
            {"tp": 2 * y + hg, "fsdp": fs - y + yy},
        )

    def is_self(hg, yy):
        return jnp.logical_and(t == 2 * y + hg, y == yy)

    def backward(hg):
        bs[hg] = lax.dot_general(
            acc[hg].astype(BF16), sel[...], (((0,), (0,)), ((), ())), preferred_element_type=F32
        ).astype(BF16)
        for yy in range(2):
            @pl.when(is_self(hg, yy))
            def _():
                br[t] = bs[hg, yy * 32:(yy + 1) * 32, :]

            @pl.when(jnp.logical_not(is_self(hg, yy)))
            def _():
                bw_send(hg, yy).start()

    def finish_early(u, carry):
        copy_a(u).wait_send()
        copy_b(u).wait_send()
        copy_y(u).wait_send()
        for dx, dy in plane:
            copy_p(u, dx, dy).wait_send()
        return carry

    def finish_ring(u, carry):
        for s in range(steps - 1):
            ring(u, s, 0, up).wait_send()
            ring(u, s, 1, down).wait_send()
        pl.when(lax.rem(u, 2) == 0)(lambda: ring(u, steps - 1, 0, up).wait_send())
        pl.when(lax.rem(u, 2) == 1)(lambda: ring(u, steps - 1, 1, down).wait_send())
        return carry

    def finish_late(u, carry):
        fo_local(u).wait()
        fo_remote(u, y).wait_send()
        fo_remote(u, 1 - y).wait_recv()
        return carry

    def each(low, high, body):
        def step(c, carry):
            body(c)
            return carry

        lax.fori_loop(low, high, step, 0)

    def start_piece(c):
        stage_d(c)
        ring_step(c, 0)

        @pl.when(c + 2 < nu)
        def _():
            stage_c(lax.rem(c + 2, nu))

    def finish_piece(c):
        arrived(c, nz - 1)
        products(c, 3)
        results(c)

    def last_steps(q, carry):
        def guarded(back, body):
            @pl.when(jnp.logical_and(q >= back, q < back + nu))
            def _():
                body(lax.rem(q + 2 * nu - back, nu))

        guarded(0, functools.partial(ring_step, s=steps - 2))
        guarded(1, functools.partial(ring_step, s=steps - 1))
        guarded(1, functools.partial(products, kk=2))
        guarded(2, finish_piece)
        pl.when(q == nu // 2 + 1)(functools.partial(backward, 0))
        return carry

    each(0, 2, stage_b)
    choose()
    each(2, nu, stage_b)
    for load in loads[1:4]:
        load.wait()
    stage_c(0)
    stage_c(1)
    each(0, nu, start_piece)
    for out in outs:
        out.start()
    og_send()
    for s in range(1, steps - 2):
        each(0, nu, functools.partial(ring_step, s=s))
        if s == 1:
            lax.fori_loop(0, nu, finish_early, 0)
            copy_x.wait_send()
        if s == 3:
            og_pass()
        if s == 4:
            og_finish()
            each(0, nu, functools.partial(products, kk=0))
        if s == 5:
            each(0, nu, functools.partial(products, kk=1))
    lax.fori_loop(0, nu + 2, last_steps, 0)
    backward(1)
    lax.fori_loop(0, nu, finish_ring, 0)
    for out in outs:
        out.wait()

    at_home = lax.div(t, 2) == y
    for x in range(4):
        @pl.when(jnp.logical_not(jnp.logical_and(at_home, t == x)))
        def _():
            remote(
                bs.at[0, pl.ds(0, 32), :], br.at[x], bw_s.at[0], bw_r.at[x], mate
            ).wait_recv()
    total = br[0].astype(F32) + br[1].astype(F32) + br[2].astype(F32) + br[3].astype(F32)
    bo[...] = total.astype(BF16)
    out_b = pltpu.make_async_copy(bo, o_bwd, out_s.at[3])
    out_b.start()

    for hg in range(2):
        for yy in range(2):
            @pl.when(jnp.logical_not(is_self(hg, yy)))
            def _():
                bw_send(hg, yy).wait_send()
    for dx in range(4):
        def og_done():
            remote(og_from, og_slot(t, y, k), og_s.at[dx], og_r.at[og_number], mate).wait_send()
        if dx == 0:
            pl.when(og_row != y)(og_done)
        else:
            og_done()
    for i in range(4):
        og_share(i).wait_send()
    lax.fori_loop(0, nu, finish_late, 0)
    out_b.wait()


def hand_over(*refs):
    ins, outs, held, came, went = refs[:5], refs[5:10], refs[10:15], refs[15], refs[16]
    reads = [pltpu.make_async_copy(ins[i], held[i], came.at[i]) for i in range(5)]
    writes = [pltpu.make_async_copy(held[i], outs[i], went.at[i]) for i in range(5)]
    for copy in reads:
        copy.start()
    for read, write in zip(reads, writes):
        read.wait()
        write.start()
    for copy in writes:
        copy.wait()


def local(master, moment_one, moment_two, grads, inputs, out_grad):
    nz = lax.axis_size("fsdp") // 2
    rows, hidden = master.shape[1:]
    tokens = inputs.shape[0]
    nu = hidden // 2 // UNIT
    steps = nz // 2
    any_spec = pl.BlockSpec(memory_space=pltpu.HBM)
    vm = pltpu.VMEM
    dma = pltpu.SemaphoreType.DMA
    results = (
        jax.ShapeDtypeStruct((rows, hidden), F32),
        jax.ShapeDtypeStruct((rows, hidden), F32),
        jax.ShapeDtypeStruct((rows, hidden), F32),
        jax.ShapeDtypeStruct((tokens, hidden), BF16),
        jax.ShapeDtypeStruct((tokens, 64 * nz), BF16),
    )
    made = pl.pallas_call(
        functools.partial(kernel, nz, nu),
        out_shape=results,
        in_specs=[any_spec] * 6,
        out_specs=[any_spec] * 5,
        scratch_shapes=[
            vm((rows, hidden), F32),
            vm((rows, hidden), F32),
            vm((rows, hidden), F32),
            vm((32, hidden), BF16),
            vm((tokens, 64 * nz), BF16),
            vm((2 * tokens, 16 * nz), BF16),
            vm((4, 2 * tokens, 64), BF16),
            vm((2, 2 * tokens, hidden // 4), BF16),
            vm((16 * nz, 64 * nz), BF16),
            vm((256, 256), BF16),
            vm((nu, 16, 2 * UNIT), BF16),
            vm((nu, 16, 2 * UNIT), BF16),
            vm((nu, 8, 2 * UNIT), F32),
            vm((nu, 16, UNIT), BF16),
            vm((nu, 16, UNIT), BF16),
            vm((nu, 16, UNIT // 2), BF16),
            vm((nu, 16, UNIT // 2), BF16),
            vm((nu, 2, 8, 256), F32),
            vm((nu, 8, 8, 256), F32),
            vm((nz, 16, nu * MSG), BF16),
            vm((nu, 2 * tokens, UNIT), F32),
            vm((nu, 2 * tokens, UNIT), BF16),
            vm((2, 16 * nz, 2 * tokens), F32),
            vm((2, 2 * tokens, 64 * nz), BF16),
            vm((4, tokens, 64 * nz), BF16),
            vm((tokens, 64 * nz), BF16),
            dma((5,)),
            dma((nu,)), dma((nu,)), dma((nu,)), dma((nu,)), dma((nu,)), dma((nu,)),
            dma((nu, 8)), dma((nu, 8)),
            dma((2, nu, steps)), dma((nu, nz)),
            dma((4,)), dma((4,)), dma((4,)), dma((4,)),
            dma, dma,
            dma((nu,)), dma((nu,)), dma((nu,)),
            dma((4,)), dma((4,)),
            dma((4,)),
        ],
        compiler_params=pltpu.CompilerParams(
            collective_id=0, has_side_effects=True, vmem_limit_bytes=VMEM_BYTES
        ),
    )(
        master.reshape(rows, hidden),
        moment_one.reshape(rows, hidden),
        moment_two.reshape(rows, hidden),
        grads.reshape(32, hidden),
        inputs,
        out_grad,
    )
    new_master, new_one, new_two, fwd, bwd = pl.pallas_call(
        hand_over,
        out_shape=results,
        in_specs=[any_spec] * 5,
        out_specs=[any_spec] * 5,
        scratch_shapes=[vm(made[i].shape, made[i].dtype) for i in range(5)] + [dma((5,)), dma((5,))],
        compiler_params=pltpu.CompilerParams(vmem_limit_bytes=VMEM_BYTES),
    )(*made)
    return (
        new_master.reshape(master.shape),
        new_one.reshape(master.shape),
        new_two.reshape(master.shape),
        fwd.reshape(1, 1, tokens, hidden),
        bwd.reshape(1, tokens, 64 * nz),
    )


def solution(mesh):
    placed = (
        P(("rep", "fsdp"), "tp", None),
        P(("rep", "fsdp"), "tp", None),
        P(("rep", "fsdp"), "tp", None),
        P("rep", None, "fsdp", "tp", None),
        P("fsdp", None),
        P("fsdp", "tp"),
    )
    return jax.shard_map(
        local,
        mesh=mesh,
        in_specs=placed,
        out_specs=(
            P(("rep", "fsdp"), "tp", None),
            P(("rep", "fsdp"), "tp", None),
            P(("rep", "fsdp"), "tp", None),
            P("rep", "tp", "fsdp", None),
            P("tp", "fsdp", "rep"),
        ),
        check_vma=False,
    )
```

```python
import functools

import jax
import jax.numpy as jnp
from jax import lax
from jax.experimental import pallas as pl
from jax.experimental.pallas import tpu as pltpu
from jax.sharding import PartitionSpec as P

beta_one = 0.9
beta_two = 0.95
learn_rate = 0.003
decay_rate = 0.1
block_width = 32

MESH = pl.DeviceIdType.MESH
F32 = jnp.float32
BF16 = jnp.bfloat16

VMEM_BYTES = 63 * 1024 * 1024
UNIT = 1792
BLOCKS = UNIT // 256
PARTS = ((0, 5), (5, 10), (10, 15), (15, 16))
MSG = UNIT + 256


def kernel(
    nz, nu,
    master, mone, mtwo, grads, inputs, ograd,
    o_master, o_one, o_two, o_fwd, o_bwd,
    m0, m1, m2, gr, xa, xs, xk, ogb, sel, ones,
    sa, ra, keep, sb, rb, ys, yr, ps, pr, g, facc, fo, acc, bs, br, bo,
    ld, sa_s, sa_r, sb_s, sb_r, ys_s, ys_r, ps_s, ps_r, ring_s, ring_r,
    og_s, og_r, sh_s, sh_r, xs_s, xs_r, fo_s, fo_r, fo_l, bw_s, bw_r, out_s,
):
    half = nu * UNIT
    rep = lax.axis_index("rep")
    fs = lax.axis_index("fsdp")
    t = lax.axis_index("tp")
    nf = 2 * nz
    yh = lax.div(rep, 2)
    k = lax.rem(rep, 2)
    z = lax.div(fs, 2)
    y = lax.rem(fs, 2)
    first_core = k == 0
    first_y = y == 0

    sibling = {"rep": rep + 1 - 2 * k}
    opposite = {"rep": lax.rem(rep + 2, 4)}
    up = {"fsdp": lax.rem(fs + 2, nf)}
    down = {"fsdp": lax.rem(fs + nf - 2, nf)}
    mate = {"fsdp": fs + 1 - 2 * y}
    plane = [(dx, dy) for dx in range(4) for dy in range(2) if (dx, dy) != (0, 0)]

    def at(dx, dy):
        where_to = {}
        if dx:
            where_to["tp"] = lax.rem(t + dx, 4)
        if dy:
            where_to["fsdp"] = fs + 1 - 2 * y
        return where_to

    def remote(src, dst, send, recv, who):
        return pltpu.make_async_remote_copy(
            src_ref=src, dst_ref=dst, send_sem=send, recv_sem=recv, device_id=who, device_id_type=MESH
        )

    def aligned(value, step):
        return pl.multiple_of(value, step)

    loads = [
        pltpu.make_async_copy(grads, gr, ld.at[0]),
        pltpu.make_async_copy(master, m0, ld.at[1]),
        pltpu.make_async_copy(mone, m1, ld.at[2]),
        pltpu.make_async_copy(mtwo, m2, ld.at[3]),
        pltpu.make_async_copy(inputs.at[:, pl.ds(aligned(rep * 1024, 1024), 1024)], xa, ld.at[4]),
    ]
    barrier = pltpu.get_barrier_semaphore()
    partners = [sibling, opposite, up, down] + [at(dx, dy) for dx, dy in plane]
    for who in partners:
        pl.semaphore_signal(barrier, inc=1, device_id=who, device_id_type=MESH)
    for load in loads:
        load.start()
    loads[0].wait()
    pl.semaphore_wait(barrier, len(partners))

    def copy_a(u):
        return remote(sa.at[u], ra.at[u], sa_s.at[u], sa_r.at[u], sibling)

    def two_groups(hi, cols):
        pair = gr[pl.ds(aligned(hi * 16, 16), 16), cols].astype(F32)
        return pair[0:8], pair[8:16]

    def stage_a(u, carry):
        for h in range(2):
            cols = pl.ds(aligned(h * half + u * UNIT, 256), UNIT)
            a0, a1 = two_groups(yh, cols)
            b0, b1 = two_groups(1 - yh, cols)
            kept = jnp.where(first_core, a1, a0)
            sent = jnp.where(first_core, b1, b0)
            sa[u, :, h * UNIT:(h + 1) * UNIT] = jnp.concatenate([kept, sent], axis=0).astype(BF16)
        copy_a(u).start()
        return carry

    lax.fori_loop(0, nu, stage_a, 0)

    my_rows = pl.ds(aligned(y * 32, 32), 32)
    copy_x = remote(xs.at[my_rows, :], xs.at[my_rows, :], xs_s, xs_r, mate)

    def choose():
        row_of = lax.broadcasted_iota(jnp.int32, (256, 256), 0)
        col_of = lax.broadcasted_iota(jnp.int32, (256, 256), 1)
        ones[...] = jnp.where((row_of >> 5) == (col_of >> 5), 1.0, 0.0).astype(BF16)
        slot = row_of >> 4
        away = (slot + 1) >> 1
        band = 2 * (jnp.where((slot & 1) == 1, z + nz - away, z + away) & (nz - 1)) + ((row_of >> 3) & 1)
        target = band * 32 + t * 8 + (row_of & 7)
        for q in range(4):
            sel[:, q * 256:(q + 1) * 256] = jnp.where(target == col_of + q * 256, 1.0, 0.0).astype(BF16)
        acc[...] = jnp.zeros_like(acc)
        loads[4].wait()
        mine = lax.dot_general(xa[...], sel[...], (((1,), (1,)), ((), ())), preferred_element_type=F32)
        xs[my_rows, :] = mine.astype(BF16)
        copy_x.start()

    def copy_b(u):
        return remote(sb.at[u], rb.at[u], sb_s.at[u], sb_r.at[u], opposite)

    def stage_b(u):
        copy_a(u).wait_recv()
        sends = []
        for h in range(2):
            cols = pl.ds(aligned(h * half + u * UNIT, 256), UNIT)
            a0, a1 = two_groups(yh, cols)
            b0, b1 = two_groups(1 - yh, cols)
            got = ra[u, :, h * UNIT:(h + 1) * UNIT].astype(F32)
            keep[u, :, h * UNIT:(h + 1) * UNIT] = jnp.where(first_core, a0, a1) + got[0:8]
            sends.append(jnp.where(first_core, b0, b1) + got[8:16])
        sb[u] = jnp.concatenate(sends, axis=0).astype(BF16)
        copy_b(u).start()

    def copy_y(u):
        return remote(ys.at[u], yr.at[u], ys_s.at[u], ys_r.at[u], mate)

    def copy_p(u, dx, dy):
        mine = t * 2 + y
        choice = y if dy == 0 else 1 - y
        return remote(ps.at[u, choice], pr.at[u, mine], ps_s.at[u, dx * 2 + dy], ps_r.at[u, mine], at(dx, dy))

    def wait_p(u, dx, dy):
        slot = lax.rem(t + dx, 4) * 2 + (y if dy == 0 else 1 - y)
        remote(ps.at[u, 0], pr.at[u, slot], ps_s.at[u, dx * 2 + dy], ps_r.at[u, slot], at(dx, dy)).wait_recv()

    scale_one = 1.0 / (1.0 - beta_one**10)
    scale_two = 1.0 / (1.0 - beta_two**10)
    sub = lax.broadcasted_iota(jnp.int32, (8, 256), 0)

    def stage_c(u):
        copy_b(u).wait_recv()
        got = rb[u].astype(F32)
        for h in range(2):
            cols = pl.ds(aligned(h * half + u * UNIT, 256), UNIT)
            grad = (keep[u, :, h * UNIT:(h + 1) * UNIT] + got[h * 8:(h + 1) * 8]) * 0.25
            new_one = beta_one * m1[:, cols] + (1.0 - beta_one) * grad
            new_two = beta_two * m2[:, cols] + (1.0 - beta_two) * grad * grad
            step_dir = new_one * scale_one / (jnp.sqrt(new_two * scale_two) + 1e-08)
            old = m0[:, cols]
            new = old - learn_rate * (step_dir + decay_rate * old)
            m0[:, cols] = new
            m1[:, cols] = new_one
            m2[:, cols] = new_two
            total = jnp.sum(jnp.abs(new), axis=0, keepdims=True)
            packed = jnp.zeros((8, 256), F32)
            for r in range(BLOCKS):
                packed = jnp.where(sub == r, total[:, r * 256:(r + 1) * 256], packed)
            ps[u, h] = packed
        pr[u, t * 2 + y] = ps[u, y]
        for dx, dy in plane:
            copy_p(u, dx, dy).start()
        other = m0[:, pl.ds(aligned((1 - y) * half + u * UNIT, 256), UNIT)]
        ys[u] = jnp.concatenate([other[:, :UNIT // 2], other[:, UNIT // 2:]], axis=0).astype(BF16)
        copy_y(u).start()

    def stage_d(u):
        for dx, dy in plane:
            wait_p(u, dx, dy)
        levels = []
        for e in range(2):
            total = pr[u, e] + pr[u, 2 + e] + pr[u, 4 + e] + pr[u, 6 + e]
            levels.append(total * (2.5 / 32.0))
        g[0, :, pl.ds(aligned(u * MSG + UNIT, 256), 256)] = jnp.concatenate(levels, axis=0).astype(BF16)
        copy_y(u).wait_recv()
        got = yr[u].astype(F32)
        theirs = jnp.concatenate([got[0:8], got[8:16]], axis=1)
        own = m0[:, pl.ds(aligned(y * half + u * UNIT, 256), UNIT)]
        even = jnp.where(first_y, own, theirs)
        odd = jnp.where(first_y, theirs, own)
        g[0, :, pl.ds(aligned(u * MSG, 128), UNIT)] = jnp.concatenate([even, odd], axis=0).astype(BF16)

    def place(c, slot):
        return g.at[slot, :, pl.ds(aligned(c * MSG, 128), MSG)]

    def ring(c, s, way, who):
        src = max(2 * s - 1, 0) if way == 0 else 2 * s
        dst = min(2 * s + 1 + way, nz - 1)
        return remote(place(c, src), place(c, dst), ring_s.at[way, c, s], ring_r.at[c, dst], who)

    def arrived(c, slot):
        remote(place(c, slot), place(c, slot), ring_s.at[0, c, 0], ring_r.at[c, slot], up).wait_recv()

    def ring_step(c, s):
        if s > 0:
            arrived(c, 2 * s - 1)
        if s < steps - 1:
            ring(c, s, 0, up).start()
            if s > 0:
                arrived(c, 2 * s)
            ring(c, s, 1, down).start()
        else:
            arrived(c, 2 * s)

            @pl.when(lax.rem(c, 2) == 0)
            def _():
                ring(c, s, 0, up).start()

            @pl.when(lax.rem(c, 2) == 1)
            def _():
                ring(c, s, 1, down).start()

    def og_slot(xsrc, ysrc, core):
        return ogb.at[lax.rem(xsrc, 2), pl.ds(aligned(ysrc * 32 + core * 16, 16), 16), :]

    og_from = ograd.at[pl.ds(aligned(k * 16, 16), 16), :]
    og_row = lax.div(t, 2)
    og_number = lax.rem(t, 2) * 2 + y

    def og_send():
        for dx in range(4):
            to = {"tp": lax.rem(t + dx, 4), "fsdp": fs - y + og_row}
            dst = og_slot(t, y, k)
            if dx == 0:
                @pl.when(og_row == y)
                def _():
                    pltpu.make_async_copy(og_from, dst, og_r.at[og_number]).start()

                @pl.when(og_row != y)
                def _():
                    remote(og_from, dst, og_s.at[dx], og_r.at[og_number], to).start()
            else:
                remote(og_from, dst, og_s.at[dx], og_r.at[og_number], to).start()

    def og_share(i):
        slot = og_slot(2 * y + i // 2, i % 2, k)
        return remote(slot, slot, sh_s.at[i], sh_r.at[i], sibling)

    def og_pass():
        for i in range(4):
            slot = og_slot(2 * y + i // 2, i % 2, k)
            local = jnp.logical_and(t == 2 * y + i // 2, y == i % 2)

            @pl.when(local)
            def _():
                pltpu.make_async_copy(og_from, slot, og_r.at[i]).wait()

            @pl.when(jnp.logical_not(local))
            def _():
                remote(og_from, slot, og_s.at[0], og_r.at[i], mate).wait_recv()

            og_share(i).start()

    def og_finish():
        for i in range(4):
            slot = og_slot(2 * y + i // 2, i % 2, 1 - k)
            remote(slot, slot, sh_s.at[i], sh_r.at[i], sibling).wait_recv()
        other_rows = pl.ds(aligned((1 - y) * 32, 32), 32)
        remote(xs.at[other_rows, :], xs.at[other_rows, :], xs_s, xs_r, mate).wait_recv()
        for kk, (low, high) in enumerate(PARTS):
            xk[kk, :, :16 * (high - low)] = xs[:, 16 * low:16 * high]

    def og_sent():
        for dx in range(4):
            def og_done():
                remote(og_from, og_slot(t, y, k), og_s.at[dx], og_r.at[og_number], mate).wait_send()
            if dx == 0:
                pl.when(og_row != y)(og_done)
            else:
                og_done()
        for i in range(4):
            og_share(i).wait_send()

    def fo_cols(u, side):
        return pl.ds(aligned(side * half + u * UNIT, 256), UNIT)

    def fo_local(u):
        return pltpu.make_async_copy(fo.at[u, my_rows, :], o_fwd.at[:, fo_cols(u, y)], fo_l.at[u])

    def fo_remote(u, side):
        rows = pl.ds(aligned((1 - y) * 32, 32), 32)
        return remote(fo.at[u, rows, :], o_fwd.at[:, fo_cols(u, side)], fo_s.at[u], fo_r.at[u], mate)

    def products(u, kk):
        low, high = PARTS[kk]
        slots, rows, bands = slice(low, high), 16 * (high - low), 2 * (high - low)
        levels = g[slots, :, pl.ds(aligned(u * MSG + UNIT, 256), 256)].astype(F32).reshape(bands, 8, 256)
        wholes = [g[slots, :, pl.ds(aligned(u * MSG + i * 256, 256), 256)].reshape(rows, 256) for i in range(BLOCKS)]
        sums = jnp.dot(jnp.abs(jnp.concatenate(wholes, axis=0)), ones[...], preferred_element_type=F32)
        hg = lax.div(u, 2)
        for i in range(BLOCKS):
            wide = wholes[i].astype(F32)
            level = jnp.broadcast_to(levels[:, i:i + 1, :], (bands, 8, 256)).reshape(rows, 256)
            band = jnp.maximum(jnp.minimum(wide, level), -level).astype(BF16)
            fwd = jnp.dot(xk[kk, :, :rows], band, preferred_element_type=F32)
            cols = slice(i * 256, (i + 1) * 256)
            if kk == 0:
                facc[u, :, cols] = fwd
            elif kk < len(PARTS) - 1:
                facc[u, :, cols] += fwd
            else:
                fo[u, :, cols] = (facc[u, :, cols] + fwd).astype(BF16)
            level = sums[i * rows:(i + 1) * rows] * (2.5 / 32.0)
            unit = jnp.maximum(jnp.minimum(wide, level), -level).astype(BF16)
            og = ogb[hg, :, pl.ds(aligned(lax.rem(u, 2) * UNIT + i * 256, 256), 256)]
            acc[hg, 16 * low:16 * high, :] += lax.dot_general(
                unit, og, (((1,), (1,)), ((), ())), preferred_element_type=F32
            )

    def results(u):
        fo_local(u).start()
        fo_remote(u, y).start()

    outs = [
        pltpu.make_async_copy(m0, o_master, out_s.at[0]),
        pltpu.make_async_copy(m1, o_one, out_s.at[1]),
        pltpu.make_async_copy(m2, o_two, out_s.at[2]),
    ]
    steps = nz // 2

    def bw_send(hg, yy):
        return remote(
            bs.at[hg, pl.ds(yy * 32, 32), :], br.at[t], bw_s.at[hg * 2 + yy], bw_r.at[t],
            {"tp": 2 * y + hg, "fsdp": fs - y + yy},
        )

    def is_self(hg, yy):
        return jnp.logical_and(t == 2 * y + hg, y == yy)

    def backward(hg):
        bs[hg] = lax.dot_general(
            acc[hg].astype(BF16), sel[...], (((0,), (0,)), ((), ())), preferred_element_type=F32
        ).astype(BF16)
        for yy in range(2):
            @pl.when(is_self(hg, yy))
            def _():
                br[t] = bs[hg, yy * 32:(yy + 1) * 32, :]

            @pl.when(jnp.logical_not(is_self(hg, yy)))
            def _():
                bw_send(hg, yy).start()

    def finish_early(u, carry):
        copy_a(u).wait_send()
        copy_b(u).wait_send()
        copy_y(u).wait_send()
        for dx, dy in plane:
            copy_p(u, dx, dy).wait_send()
        return carry

    def sent(u, low, high):
        for s in range(low, high):
            ring(u, s, 0, up).wait_send()
            ring(u, s, 1, down).wait_send()

    def sent_last(u, carry):
        sent(u, 4, steps - 1)
        pl.when(lax.rem(u, 2) == 0)(lambda: ring(u, steps - 1, 0, up).wait_send())
        pl.when(lax.rem(u, 2) == 1)(lambda: ring(u, steps - 1, 1, down).wait_send())
        return carry

    def finish_late(u, carry):
        fo_local(u).wait()
        fo_remote(u, y).wait_send()
        fo_remote(u, 1 - y).wait_recv()
        return carry

    def each(low, high, body):
        def step(c, carry):
            body(c)
            return carry

        lax.fori_loop(low, high, step, 0)

    def start_piece(c):
        stage_d(c)
        ring_step(c, 0)

        @pl.when(c + 3 < nu)
        def _():
            stage_c(lax.rem(c + 3, nu))

    def finish_piece(c):
        arrived(c, nz - 1)
        products(c, 3)
        results(c)

    def step_and_waits(c, s):
        ring_step(c, s)
        if s == 2:
            finish_early(c, 0)
        if s == 3:
            sent(c, 0, 2)

    def early_sent(c, s):
        ring_step(c, s)
        products(c, 2)
        sent(c, 2, 4)

    def step_and_part(c, s, kk):
        ring_step(c, s)
        products(c, kk)

    def last_steps(q, carry):
        def guarded(back, body):
            @pl.when(jnp.logical_and(q >= back, q < back + nu))
            def _():
                body(lax.rem(q + 2 * nu - back, nu))

        guarded(0, functools.partial(step_and_part, s=steps - 3, kk=1))
        guarded(1, functools.partial(ring_step, s=steps - 2))
        guarded(2, functools.partial(early_sent, s=steps - 1))
        guarded(3, finish_piece)
        pl.when(q == nu // 2 + 2)(functools.partial(backward, 0))
        return carry

    each(0, 2, stage_b)
    choose()
    each(2, nu, stage_b)
    for load in loads[1:4]:
        load.wait()
    each(0, 3, stage_c)
    each(0, nu, start_piece)
    for out in outs:
        out.start()
    og_send()
    for s in range(1, steps - 3):
        if s == steps - 4:
            og_finish()
            og_sent()
            copy_x.wait_send()
        if s >= steps - 4:
            each(0, nu, functools.partial(step_and_part, s=s, kk=s - steps + 4))
        else:
            each(0, nu, functools.partial(step_and_waits, s=s))
        if s == 3:
            og_pass()
    lax.fori_loop(0, nu + 3, last_steps, 0)
    backward(1)
    lax.fori_loop(0, nu, sent_last, 0)
    for out in outs:
        out.wait()

    at_home = lax.div(t, 2) == y
    for x in range(4):
        @pl.when(jnp.logical_not(jnp.logical_and(at_home, t == x)))
        def _():
            remote(
                bs.at[0, pl.ds(0, 32), :], br.at[x], bw_s.at[0], bw_r.at[x], mate
            ).wait_recv()
    total = br[0].astype(F32) + br[1].astype(F32) + br[2].astype(F32) + br[3].astype(F32)
    bo[...] = total.astype(BF16)
    out_b = pltpu.make_async_copy(bo, o_bwd, out_s.at[3])
    out_b.start()

    for hg in range(2):
        for yy in range(2):
            @pl.when(jnp.logical_not(is_self(hg, yy)))
            def _():
                bw_send(hg, yy).wait_send()
    lax.fori_loop(0, nu, finish_late, 0)
    out_b.wait()


def hand_over(*refs):
    ins, outs, held, came, went = refs[:5], refs[5:10], refs[10:15], refs[15], refs[16]
    reads = [pltpu.make_async_copy(ins[i], held[i], came.at[i]) for i in range(5)]
    writes = [pltpu.make_async_copy(held[i], outs[i], went.at[i]) for i in range(5)]
    for copy in reads:
        copy.start()
    for read, write in zip(reads, writes):
        read.wait()
        write.start()
    for copy in writes:
        copy.wait()


def local(master, moment_one, moment_two, grads, inputs, out_grad):
    nz = lax.axis_size("fsdp") // 2
    rows, hidden = master.shape[1:]
    tokens = inputs.shape[0]
    nu = hidden // 2 // UNIT
    steps = nz // 2
    any_spec = pl.BlockSpec(memory_space=pltpu.HBM)
    vm = pltpu.VMEM
    dma = pltpu.SemaphoreType.DMA
    results = (
        jax.ShapeDtypeStruct((rows, hidden), F32),
        jax.ShapeDtypeStruct((rows, hidden), F32),
        jax.ShapeDtypeStruct((rows, hidden), F32),
        jax.ShapeDtypeStruct((tokens, hidden), BF16),
        jax.ShapeDtypeStruct((tokens, 64 * nz), BF16),
    )
    made = pl.pallas_call(
        functools.partial(kernel, nz, nu),
        out_shape=results,
        in_specs=[any_spec] * 6,
        out_specs=[any_spec] * 5,
        scratch_shapes=[
            vm((rows, hidden), F32),
            vm((rows, hidden), F32),
            vm((rows, hidden), F32),
            vm((32, hidden), BF16),
            vm((tokens, 64 * nz), BF16),
            vm((2 * tokens, 16 * nz), BF16),
            vm((4, 2 * tokens, 80), BF16),
            vm((2, 2 * tokens, hidden // 4), BF16),
            vm((16 * nz, 64 * nz), BF16),
            vm((256, 256), BF16),
            vm((nu, 16, 2 * UNIT), BF16),
            vm((nu, 16, 2 * UNIT), BF16),
            vm((nu, 8, 2 * UNIT), F32),
            vm((nu, 16, UNIT), BF16),
            vm((nu, 16, UNIT), BF16),
            vm((nu, 16, UNIT // 2), BF16),
            vm((nu, 16, UNIT // 2), BF16),
            vm((nu, 2, 8, 256), F32),
            vm((nu, 8, 8, 256), F32),
            vm((nz, 16, nu * MSG), BF16),
            vm((nu, 2 * tokens, UNIT), F32),
            vm((nu, 2 * tokens, UNIT), BF16),
            vm((2, 16 * nz, 2 * tokens), F32),
            vm((2, 2 * tokens, 64 * nz), BF16),
            vm((4, tokens, 64 * nz), BF16),
            vm((tokens, 64 * nz), BF16),
            dma((5,)),
            dma((nu,)), dma((nu,)), dma((nu,)), dma((nu,)), dma((nu,)), dma((nu,)),
            dma((nu, 8)), dma((nu, 8)),
            dma((2, nu, steps)), dma((nu, nz)),
            dma((4,)), dma((4,)), dma((4,)), dma((4,)),
            dma, dma,
            dma((nu,)), dma((nu,)), dma((nu,)),
            dma((4,)), dma((4,)),
            dma((4,)),
        ],
        compiler_params=pltpu.CompilerParams(
            collective_id=0, has_side_effects=True, vmem_limit_bytes=VMEM_BYTES
        ),
    )(
        master.reshape(rows, hidden),
        moment_one.reshape(rows, hidden),
        moment_two.reshape(rows, hidden),
        grads.reshape(32, hidden),
        inputs,
        out_grad,
    )
    new_master, new_one, new_two, fwd, bwd = pl.pallas_call(
        hand_over,
        out_shape=results,
        in_specs=[any_spec] * 5,
        out_specs=[any_spec] * 5,
        scratch_shapes=[vm(made[i].shape, made[i].dtype) for i in range(5)] + [dma((5,)), dma((5,))],
        compiler_params=pltpu.CompilerParams(vmem_limit_bytes=VMEM_BYTES),
    )(*made)
    return (
        new_master.reshape(master.shape),
        new_one.reshape(master.shape),
        new_two.reshape(master.shape),
        fwd.reshape(1, 1, tokens, hidden),
        bwd.reshape(1, tokens, 64 * nz),
    )


def solution(mesh):
    placed = (
        P(("rep", "fsdp"), "tp", None),
        P(("rep", "fsdp"), "tp", None),
        P(("rep", "fsdp"), "tp", None),
        P("rep", None, "fsdp", "tp", None),
        P("fsdp", None),
        P("fsdp", "tp"),
    )
    return jax.shard_map(
        local,
        mesh=mesh,
        in_specs=placed,
        out_specs=(
            P(("rep", "fsdp"), "tp", None),
            P(("rep", "fsdp"), "tp", None),
            P(("rep", "fsdp"), "tp", None),
            P("rep", "tp", "fsdp", None),
            P("tp", "fsdp", "rep"),
        ),
        check_vma=False,
    )
```

```python
import functools

import jax
import jax.numpy as jnp
from jax import lax
from jax.experimental import pallas as pl
from jax.experimental.pallas import tpu as pltpu
from jax.sharding import PartitionSpec as P

beta_one = 0.9
beta_two = 0.95
learn_rate = 0.003
decay_rate = 0.1
block_width = 32

MESH = pl.DeviceIdType.MESH
F32 = jnp.float32
BF16 = jnp.bfloat16

VMEM_BYTES = 63 * 1024 * 1024
UNIT = 1792
BLOCKS = UNIT // 256
PARTS = ((0, 5), (5, 10), (10, 15), (15, 16))
MSG = UNIT + 256


def kernel(
    nz, nu,
    master, mone, mtwo, grads, inputs, ograd,
    o_master, o_one, o_two, o_fwd, o_bwd,
    m0, m1, m2, gr, xa, xs, xk, ogb, sel, spread_to, eye, ones,
    sa, ra, keep, sb, rb, ys, yr, ps, pr, g, facc, fo, acc, bs, br, bo,
    ld, sa_s, sa_r, sb_s, sb_r, ys_s, ys_r, ps_s, ps_r, ring_s, ring_r,
    og_s, og_r, sh_s, sh_r, xs_s, xs_r, fo_s, fo_r, fo_l, bw_s, bw_r, out_s,
):
    half = nu * UNIT
    rep = lax.axis_index("rep")
    fs = lax.axis_index("fsdp")
    t = lax.axis_index("tp")
    nf = 2 * nz
    yh = lax.div(rep, 2)
    k = lax.rem(rep, 2)
    z = lax.div(fs, 2)
    y = lax.rem(fs, 2)
    first_core = k == 0
    first_y = y == 0

    sibling = {"rep": rep + 1 - 2 * k}
    opposite = {"rep": lax.rem(rep + 2, 4)}
    up = {"fsdp": lax.rem(fs + 2, nf)}
    down = {"fsdp": lax.rem(fs + nf - 2, nf)}
    mate = {"fsdp": fs + 1 - 2 * y}
    plane = [(dx, dy) for dx in range(4) for dy in range(2) if (dx, dy) != (0, 0)]

    def at(dx, dy):
        where_to = {}
        if dx:
            where_to["tp"] = lax.rem(t + dx, 4)
        if dy:
            where_to["fsdp"] = fs + 1 - 2 * y
        return where_to

    def remote(src, dst, send, recv, who):
        return pltpu.make_async_remote_copy(
            src_ref=src, dst_ref=dst, send_sem=send, recv_sem=recv, device_id=who, device_id_type=MESH
        )

    def aligned(value, step):
        return pl.multiple_of(value, step)

    loads = [
        pltpu.make_async_copy(grads, gr, ld.at[0]),
        pltpu.make_async_copy(master, m0, ld.at[1]),
        pltpu.make_async_copy(mone, m1, ld.at[2]),
        pltpu.make_async_copy(mtwo, m2, ld.at[3]),
        pltpu.make_async_copy(inputs.at[:, pl.ds(aligned(rep * 1024, 1024), 1024)], xa, ld.at[4]),
    ]
    barrier = pltpu.get_barrier_semaphore()
    partners = [sibling, opposite, up, down] + [at(dx, dy) for dx, dy in plane]
    for who in partners:
        pl.semaphore_signal(barrier, inc=1, device_id=who, device_id_type=MESH)
    for load in loads:
        load.start()
    loads[0].wait()
    pl.semaphore_wait(barrier, len(partners))

    def copy_a(u):
        return remote(sa.at[u], ra.at[u], sa_s.at[u], sa_r.at[u], sibling)

    def two_groups(hi, cols):
        pair = gr[pl.ds(aligned(hi * 16, 16), 16), cols].astype(F32)
        return pair[0:8], pair[8:16]

    def stage_a(u, carry):
        for h in range(2):
            cols = pl.ds(aligned(h * half + u * UNIT, 256), UNIT)
            a0, a1 = two_groups(yh, cols)
            b0, b1 = two_groups(1 - yh, cols)
            kept = jnp.where(first_core, a1, a0)
            sent = jnp.where(first_core, b1, b0)
            sa[u, :, h * UNIT:(h + 1) * UNIT] = jnp.concatenate([kept, sent], axis=0).astype(BF16)
        copy_a(u).start()
        return carry

    lax.fori_loop(0, nu, stage_a, 0)

    my_rows = pl.ds(aligned(y * 32, 32), 32)
    copy_x = remote(xs.at[my_rows, :], xs.at[my_rows, :], xs_s, xs_r, mate)

    def place_columns(ref, x):
        row_of = lax.broadcasted_iota(jnp.int32, (256, 256), 0)
        col_of = lax.broadcasted_iota(jnp.int32, (256, 256), 1)
        slot = row_of >> 4
        away = (slot + 1) >> 1
        band = 2 * (jnp.where((slot & 1) == 1, z + nz - away, z + away) & (nz - 1)) + ((row_of >> 3) & 1)
        target = band * 32 + x * 8 + (row_of & 7)
        for q in range(4):
            ref[:, q * 256:(q + 1) * 256] = jnp.where(target == col_of + q * 256, 1.0, 0.0).astype(BF16)

    def prepare_spread(x):
        place_columns(spread_to.at[x], x)
        if x == 3:
            row_of = lax.broadcasted_iota(jnp.int32, (256, 256), 0)
            col_of = lax.broadcasted_iota(jnp.int32, (256, 256), 1)
            eye[...] = jnp.where(row_of == col_of, 1.0, 0.0).astype(BF16)

    def choose():
        row_of = lax.broadcasted_iota(jnp.int32, (256, 256), 0)
        col_of = lax.broadcasted_iota(jnp.int32, (256, 256), 1)
        ones[...] = jnp.where((row_of >> 5) == (col_of >> 5), 1.0, 0.0).astype(BF16)
        place_columns(sel, t)
        acc[...] = jnp.zeros_like(acc)
        loads[4].wait()
        mine = lax.dot_general(xa[...], sel[...], (((1,), (1,)), ((), ())), preferred_element_type=F32)
        xs[my_rows, :] = mine.astype(BF16)
        copy_x.start()

    def copy_b(u):
        return remote(sb.at[u], rb.at[u], sb_s.at[u], sb_r.at[u], opposite)

    def stage_b(u):
        copy_a(u).wait_recv()
        sends = []
        for h in range(2):
            cols = pl.ds(aligned(h * half + u * UNIT, 256), UNIT)
            a0, a1 = two_groups(yh, cols)
            b0, b1 = two_groups(1 - yh, cols)
            got = ra[u, :, h * UNIT:(h + 1) * UNIT].astype(F32)
            keep[u, :, h * UNIT:(h + 1) * UNIT] = jnp.where(first_core, a0, a1) + got[0:8]
            sends.append(jnp.where(first_core, b0, b1) + got[8:16])
        sb[u] = jnp.concatenate(sends, axis=0).astype(BF16)
        copy_b(u).start()

    def copy_y(u):
        return remote(ys.at[u], yr.at[u], ys_s.at[u], ys_r.at[u], mate)

    def copy_p(u, dx, dy):
        mine = t * 2 + y
        choice = y if dy == 0 else 1 - y
        return remote(ps.at[u, choice], pr.at[u, mine], ps_s.at[u, dx * 2 + dy], ps_r.at[u, mine], at(dx, dy))

    def wait_p(u, dx, dy):
        slot = lax.rem(t + dx, 4) * 2 + (y if dy == 0 else 1 - y)
        remote(ps.at[u, 0], pr.at[u, slot], ps_s.at[u, dx * 2 + dy], ps_r.at[u, slot], at(dx, dy)).wait_recv()

    scale_one = 1.0 / (1.0 - beta_one**10)
    scale_two = 1.0 / (1.0 - beta_two**10)
    sub = lax.broadcasted_iota(jnp.int32, (8, 256), 0)

    def stage_c(u):
        copy_b(u).wait_recv()
        got = rb[u].astype(F32)
        for h in range(2):
            cols = pl.ds(aligned(h * half + u * UNIT, 256), UNIT)
            grad = (keep[u, :, h * UNIT:(h + 1) * UNIT] + got[h * 8:(h + 1) * 8]) * 0.25
            new_one = beta_one * m1[:, cols] + (1.0 - beta_one) * grad
            new_two = beta_two * m2[:, cols] + (1.0 - beta_two) * grad * grad
            step_dir = new_one * scale_one / (jnp.sqrt(new_two * scale_two) + 1e-08)
            old = m0[:, cols]
            new = old - learn_rate * (step_dir + decay_rate * old)
            m0[:, cols] = new
            m1[:, cols] = new_one
            m2[:, cols] = new_two
            total = jnp.sum(jnp.abs(new), axis=0, keepdims=True)
            packed = jnp.zeros((8, 256), F32)
            for r in range(BLOCKS):
                packed = jnp.where(sub == r, total[:, r * 256:(r + 1) * 256], packed)
            ps[u, h] = packed
        pr[u, t * 2 + y] = ps[u, y]
        for dx, dy in plane:
            copy_p(u, dx, dy).start()
        other = m0[:, pl.ds(aligned((1 - y) * half + u * UNIT, 256), UNIT)]
        ys[u] = jnp.concatenate([other[:, :UNIT // 2], other[:, UNIT // 2:]], axis=0).astype(BF16)
        copy_y(u).start()

    def stage_d(u):
        for dx, dy in plane:
            wait_p(u, dx, dy)
        levels = []
        for e in range(2):
            total = pr[u, e] + pr[u, 2 + e] + pr[u, 4 + e] + pr[u, 6 + e]
            levels.append(total * (2.5 / 32.0))
        g[0, :, pl.ds(aligned(u * MSG + UNIT, 256), 256)] = jnp.concatenate(levels, axis=0).astype(BF16)
        copy_y(u).wait_recv()
        got = yr[u].astype(F32)
        theirs = jnp.concatenate([got[0:8], got[8:16]], axis=1)
        own = m0[:, pl.ds(aligned(y * half + u * UNIT, 256), UNIT)]
        even = jnp.where(first_y, own, theirs)
        odd = jnp.where(first_y, theirs, own)
        g[0, :, pl.ds(aligned(u * MSG, 128), UNIT)] = jnp.concatenate([even, odd], axis=0).astype(BF16)

    def place(c, slot):
        return g.at[slot, :, pl.ds(aligned(c * MSG, 128), MSG)]

    def ring(c, s, way, who):
        src = max(2 * s - 1, 0) if way == 0 else 2 * s
        dst = min(2 * s + 1 + way, nz - 1)
        return remote(place(c, src), place(c, dst), ring_s.at[way, c, s], ring_r.at[c, dst], who)

    def arrived(c, slot):
        remote(place(c, slot), place(c, slot), ring_s.at[0, c, 0], ring_r.at[c, slot], up).wait_recv()

    def ring_step(c, s):
        if s > 0:
            arrived(c, 2 * s - 1)
        if s < steps - 1:
            ring(c, s, 0, up).start()
            if s > 0:
                arrived(c, 2 * s)
            ring(c, s, 1, down).start()
        else:
            arrived(c, 2 * s)

            @pl.when(lax.rem(c, 2) == 0)
            def _():
                ring(c, s, 0, up).start()

            @pl.when(lax.rem(c, 2) == 1)
            def _():
                ring(c, s, 1, down).start()

    def og_slot(xsrc, ysrc, core):
        return ogb.at[lax.rem(xsrc, 2), pl.ds(aligned(ysrc * 32 + core * 16, 16), 16), :]

    og_from = ograd.at[pl.ds(aligned(k * 16, 16), 16), :]
    og_row = lax.div(t, 2)
    og_number = lax.rem(t, 2) * 2 + y

    def og_send():
        for dx in range(4):
            to = {"tp": lax.rem(t + dx, 4), "fsdp": fs - y + og_row}
            dst = og_slot(t, y, k)
            if dx == 0:
                @pl.when(og_row == y)
                def _():
                    pltpu.make_async_copy(og_from, dst, og_r.at[og_number]).start()

                @pl.when(og_row != y)
                def _():
                    remote(og_from, dst, og_s.at[dx], og_r.at[og_number], to).start()
            else:
                remote(og_from, dst, og_s.at[dx], og_r.at[og_number], to).start()

    def og_share(i):
        slot = og_slot(2 * y + i // 2, i % 2, k)
        return remote(slot, slot, sh_s.at[i], sh_r.at[i], sibling)

    def og_pass():
        for i in range(4):
            slot = og_slot(2 * y + i // 2, i % 2, k)
            local = jnp.logical_and(t == 2 * y + i // 2, y == i % 2)

            @pl.when(local)
            def _():
                pltpu.make_async_copy(og_from, slot, og_r.at[i]).wait()

            @pl.when(jnp.logical_not(local))
            def _():
                remote(og_from, slot, og_s.at[0], og_r.at[i], mate).wait_recv()

            og_share(i).start()

    def og_finish():
        for i in range(4):
            slot = og_slot(2 * y + i // 2, i % 2, 1 - k)
            remote(slot, slot, sh_s.at[i], sh_r.at[i], sibling).wait_recv()
        other_rows = pl.ds(aligned((1 - y) * 32, 32), 32)
        remote(xs.at[other_rows, :], xs.at[other_rows, :], xs_s, xs_r, mate).wait_recv()
        for kk, (low, high) in enumerate(PARTS):
            xk[kk, :, :16 * (high - low)] = xs[:, 16 * low:16 * high]

    def og_sent():
        for dx in range(4):
            def og_done():
                remote(og_from, og_slot(t, y, k), og_s.at[dx], og_r.at[og_number], mate).wait_send()
            if dx == 0:
                pl.when(og_row != y)(og_done)
            else:
                og_done()
        for i in range(4):
            og_share(i).wait_send()

    def fo_cols(u, side):
        return pl.ds(aligned(side * half + u * UNIT, 256), UNIT)

    def fo_local(u):
        return pltpu.make_async_copy(fo.at[u, my_rows, :], o_fwd.at[:, fo_cols(u, y)], fo_l.at[u])

    def fo_remote(u, side):
        rows = pl.ds(aligned((1 - y) * 32, 32), 32)
        return remote(fo.at[u, rows, :], o_fwd.at[:, fo_cols(u, side)], fo_s.at[u], fo_r.at[u], mate)

    def products(u, kk):
        low, high = PARTS[kk]
        slots, rows, bands = slice(low, high), 16 * (high - low), 2 * (high - low)
        levels = g[slots, :, pl.ds(aligned(u * MSG + UNIT, 256), 256)].astype(F32).reshape(bands, 8, 256)
        wholes = [g[slots, :, pl.ds(aligned(u * MSG + i * 256, 256), 256)].reshape(rows, 256) for i in range(BLOCKS)]
        sums = jnp.dot(jnp.abs(jnp.concatenate(wholes, axis=0)), ones[...], preferred_element_type=F32)
        hg = lax.div(u, 2)
        for i in range(BLOCKS):
            wide = wholes[i].astype(F32)
            level = jnp.broadcast_to(levels[:, i:i + 1, :], (bands, 8, 256)).reshape(rows, 256)
            band = jnp.maximum(jnp.minimum(wide, level), -level).astype(BF16)
            fwd = jnp.dot(xk[kk, :, :rows], band, preferred_element_type=F32)
            cols = slice(i * 256, (i + 1) * 256)
            if kk == 0:
                facc[u, :, cols] = fwd
            elif kk < len(PARTS) - 1:
                facc[u, :, cols] += fwd
            else:
                fo[u, :, cols] = (facc[u, :, cols] + fwd).astype(BF16)
            level = sums[i * rows:(i + 1) * rows] * (2.5 / 32.0)
            unit = jnp.maximum(jnp.minimum(wide, level), -level).astype(BF16)
            og = ogb[hg, :, pl.ds(aligned(lax.rem(u, 2) * UNIT + i * 256, 256), 256)]
            acc[hg, 16 * low:16 * high, :] += lax.dot_general(
                unit, og, (((1,), (1,)), ((), ())), preferred_element_type=F32
            )

    def results(u):
        fo_local(u).start()
        fo_remote(u, y).start()

    outs = [
        pltpu.make_async_copy(m0, o_master, out_s.at[0]),
        pltpu.make_async_copy(m1, o_one, out_s.at[1]),
        pltpu.make_async_copy(m2, o_two, out_s.at[2]),
    ]
    steps = nz // 2

    def bw_send(hg, yy):
        return remote(
            bs.at[hg, pl.ds(yy * 32, 32), :], br.at[t], bw_s.at[hg * 2 + yy], bw_r.at[t],
            {"tp": 2 * y + hg, "fsdp": fs - y + yy},
        )

    def is_self(hg, yy):
        return jnp.logical_and(t == 2 * y + hg, y == yy)

    def backward(hg):
        bs[hg] = lax.dot_general(
            acc[hg].astype(BF16), eye[...], (((0,), (0,)), ((), ())), preferred_element_type=F32
        ).astype(BF16)
        for yy in range(2):
            @pl.when(is_self(hg, yy))
            def _():
                br[t] = bs[hg, yy * 32:(yy + 1) * 32, :]

            @pl.when(jnp.logical_not(is_self(hg, yy)))
            def _():
                bw_send(hg, yy).start()

    def finish_early(u, carry):
        copy_a(u).wait_send()
        copy_b(u).wait_send()
        copy_y(u).wait_send()
        for dx, dy in plane:
            copy_p(u, dx, dy).wait_send()
        return carry

    def sent(u, low, high):
        for s in range(low, high):
            ring(u, s, 0, up).wait_send()
            ring(u, s, 1, down).wait_send()

    def sent_last(u, carry):
        sent(u, 4, steps - 1)
        pl.when(lax.rem(u, 2) == 0)(lambda: ring(u, steps - 1, 0, up).wait_send())
        pl.when(lax.rem(u, 2) == 1)(lambda: ring(u, steps - 1, 1, down).wait_send())
        return carry

    def finish_late(u, carry):
        fo_local(u).wait()
        fo_remote(u, y).wait_send()
        fo_remote(u, 1 - y).wait_recv()
        return carry

    def each(low, high, body):
        def step(c, carry):
            body(c)
            return carry

        lax.fori_loop(low, high, step, 0)

    def start_piece(c):
        stage_d(c)
        ring_step(c, 0)

        @pl.when(c + 3 < nu)
        def _():
            stage_c(lax.rem(c + 3, nu))

    def finish_piece(c):
        arrived(c, nz - 1)
        products(c, 3)
        pl.when(c == nu - 1)(functools.partial(backward, 1))
        results(c)

    def step_and_waits(c, s):
        ring_step(c, s)
        if s == 2:
            finish_early(c, 0)
        if s == 3:
            sent(c, 0, 2)

    def early_sent(c, s):
        ring_step(c, s)
        products(c, 2)
        sent(c, 2, 4)

    def step_and_part(c, s, kk):
        ring_step(c, s)
        products(c, kk)

    def last_steps(q, carry):
        def guarded(back, body):
            @pl.when(jnp.logical_and(q >= back, q < back + nu))
            def _():
                body(lax.rem(q + 2 * nu - back, nu))

        guarded(0, functools.partial(step_and_part, s=steps - 3, kk=1))
        guarded(1, functools.partial(ring_step, s=steps - 2))
        guarded(2, functools.partial(early_sent, s=steps - 1))
        guarded(3, finish_piece)
        pl.when(q == nu // 2 + 2)(functools.partial(backward, 0))
        return carry

    each(0, 2, stage_b)
    choose()
    each(2, nu, stage_b)
    for load in loads[1:4]:
        load.wait()
    each(0, 3, stage_c)
    each(0, nu, start_piece)
    for out in outs:
        out.start()
    og_send()
    for s in range(1, steps - 3):
        if s == steps - 4:
            og_finish()
            og_sent()
            copy_x.wait_send()
        if s >= steps - 4:
            each(0, nu, functools.partial(step_and_part, s=s, kk=s - steps + 4))
        else:
            each(0, nu, functools.partial(step_and_waits, s=s))
        if s in (1, 2):
            prepare_spread(2 * s - 2)
            prepare_spread(2 * s - 1)
        if s == 3:
            og_pass()
    lax.fori_loop(0, nu + 3, last_steps, 0)
    lax.fori_loop(0, nu, sent_last, 0)
    for out in outs:
        out.wait()

    at_home = lax.div(t, 2) == y
    for x in range(4):
        @pl.when(jnp.logical_not(jnp.logical_and(at_home, t == x)))
        def _():
            remote(
                bs.at[0, pl.ds(0, 32), :], br.at[x], bw_s.at[0], bw_r.at[x], mate
            ).wait_recv()
    total = jnp.dot(br[0], spread_to[0], preferred_element_type=F32)
    for x in range(1, 4):
        total += jnp.dot(br[x], spread_to[x], preferred_element_type=F32)
    bo[...] = total.astype(BF16)
    out_b = pltpu.make_async_copy(bo, o_bwd, out_s.at[3])
    out_b.start()

    for hg in range(2):
        for yy in range(2):
            @pl.when(jnp.logical_not(is_self(hg, yy)))
            def _():
                bw_send(hg, yy).wait_send()
    lax.fori_loop(0, nu, finish_late, 0)
    out_b.wait()


def hand_over(*refs):
    ins, outs, held, came, went = refs[:5], refs[5:10], refs[10:15], refs[15], refs[16]
    reads = [pltpu.make_async_copy(ins[i], held[i], came.at[i]) for i in range(5)]
    writes = [pltpu.make_async_copy(held[i], outs[i], went.at[i]) for i in range(5)]
    for copy in reads:
        copy.start()
    for read, write in zip(reads, writes):
        read.wait()
        write.start()
    for copy in writes:
        copy.wait()


def local(master, moment_one, moment_two, grads, inputs, out_grad):
    nz = lax.axis_size("fsdp") // 2
    rows, hidden = master.shape[1:]
    tokens = inputs.shape[0]
    nu = hidden // 2 // UNIT
    steps = nz // 2
    any_spec = pl.BlockSpec(memory_space=pltpu.HBM)
    vm = pltpu.VMEM
    dma = pltpu.SemaphoreType.DMA
    results = (
        jax.ShapeDtypeStruct((rows, hidden), F32),
        jax.ShapeDtypeStruct((rows, hidden), F32),
        jax.ShapeDtypeStruct((rows, hidden), F32),
        jax.ShapeDtypeStruct((tokens, hidden), BF16),
        jax.ShapeDtypeStruct((tokens, 64 * nz), BF16),
    )
    made = pl.pallas_call(
        functools.partial(kernel, nz, nu),
        out_shape=results,
        in_specs=[any_spec] * 6,
        out_specs=[any_spec] * 5,
        scratch_shapes=[
            vm((rows, hidden), F32),
            vm((rows, hidden), F32),
            vm((rows, hidden), F32),
            vm((32, hidden), BF16),
            vm((tokens, 64 * nz), BF16),
            vm((2 * tokens, 16 * nz), BF16),
            vm((4, 2 * tokens, 80), BF16),
            vm((2, 2 * tokens, hidden // 4), BF16),
            vm((16 * nz, 64 * nz), BF16),
            vm((4, 16 * nz, 64 * nz), BF16),
            vm((256, 256), BF16),
            vm((256, 256), BF16),
            vm((nu, 16, 2 * UNIT), BF16),
            vm((nu, 16, 2 * UNIT), BF16),
            vm((nu, 8, 2 * UNIT), F32),
            vm((nu, 16, UNIT), BF16),
            vm((nu, 16, UNIT), BF16),
            vm((nu, 16, UNIT // 2), BF16),
            vm((nu, 16, UNIT // 2), BF16),
            vm((nu, 2, 8, 256), F32),
            vm((nu, 8, 8, 256), F32),
            vm((nz, 16, nu * MSG), BF16),
            vm((nu, 2 * tokens, UNIT), F32),
            vm((nu, 2 * tokens, UNIT), BF16),
            vm((2, 16 * nz, 2 * tokens), F32),
            vm((2, 2 * tokens, 16 * nz), BF16),
            vm((4, tokens, 16 * nz), BF16),
            vm((tokens, 64 * nz), BF16),
            dma((5,)),
            dma((nu,)), dma((nu,)), dma((nu,)), dma((nu,)), dma((nu,)), dma((nu,)),
            dma((nu, 8)), dma((nu, 8)),
            dma((2, nu, steps)), dma((nu, nz)),
            dma((4,)), dma((4,)), dma((4,)), dma((4,)),
            dma, dma,
            dma((nu,)), dma((nu,)), dma((nu,)),
            dma((4,)), dma((4,)),
            dma((4,)),
        ],
        compiler_params=pltpu.CompilerParams(
            collective_id=0, has_side_effects=True, vmem_limit_bytes=VMEM_BYTES
        ),
    )(
        master.reshape(rows, hidden),
        moment_one.reshape(rows, hidden),
        moment_two.reshape(rows, hidden),
        grads.reshape(32, hidden),
        inputs,
        out_grad,
    )
    new_master, new_one, new_two, fwd, bwd = pl.pallas_call(
        hand_over,
        out_shape=results,
        in_specs=[any_spec] * 5,
        out_specs=[any_spec] * 5,
        scratch_shapes=[vm(made[i].shape, made[i].dtype) for i in range(5)] + [dma((5,)), dma((5,))],
        compiler_params=pltpu.CompilerParams(vmem_limit_bytes=VMEM_BYTES),
    )(*made)
    return (
        new_master.reshape(master.shape),
        new_one.reshape(master.shape),
        new_two.reshape(master.shape),
        fwd.reshape(1, 1, tokens, hidden),
        bwd.reshape(1, tokens, 64 * nz),
    )


def solution(mesh):
    placed = (
        P(("rep", "fsdp"), "tp", None),
        P(("rep", "fsdp"), "tp", None),
        P(("rep", "fsdp"), "tp", None),
        P("rep", None, "fsdp", "tp", None),
        P("fsdp", None),
        P("fsdp", "tp"),
    )
    return jax.shard_map(
        local,
        mesh=mesh,
        in_specs=placed,
        out_specs=(
            P(("rep", "fsdp"), "tp", None),
            P(("rep", "fsdp"), "tp", None),
            P(("rep", "fsdp"), "tp", None),
            P("rep", "tp", "fsdp", None),
            P("tp", "fsdp", "rep"),
        ),
        check_vma=False,
    )
```
